512 devices in a mesh: inst: 64 (over y, x, core), tp: 8 (over z).
Axes of the slice: x: 4, y: 8, z: 8, core: 2. Of those that a mesh axis runs over, the one named last changes fastest.
Arguments:
- query: bfloat16 [4096, 64, 128], P('inst', 'tp'), may hold values from -8 to 8
- key_cache: bfloat16 [16384, 8, 128], P('inst', 'tp'), may hold values from -8 to 8
- value_cache: bfloat16 [16384, 8, 128], P('inst', 'tp'), may hold values from -6 to 6
- span_keys: bfloat16 [4096, 8, 128], P('inst', 'tp'), may hold values from -8 to 8
- span_values: bfloat16 [4096, 8, 128], P('inst', 'tp'), may hold values from -6 to 6
- live_pages: int32 [64], P('inst'), may hold values from 24 to 32
- routes: int32 [2048, 1], P('inst'), may hold values from 0 to 63; in each aligned block of 32 rows (0 to 31, 32 to 63, ...) no two rows name the same one
- decode_query: bfloat16 [64, 128], P('tp'), may hold values from -8 to 8
- new_key: bfloat16 [8, 128], P('tp'), may hold values from -8 to 8
- new_value: bfloat16 [8, 128], P('tp'), may hold values from -6 to 6
- w_out: bfloat16 [8192, 8192], P('tp', 'inst'), may hold values from -0.0625 to 0.0625
Outputs:
- span_out: bfloat16 [4096, 64, 128], P('inst', 'tp')
- held_keys: bfloat16 [4096, 8, 8, 128], P('inst', None, 'tp')
- held_values: bfloat16 [4096, 8, 8, 128], P('inst', None, 'tp')
- held_pages: int32 [4096], P('inst')
- decoded: bfloat16 [1, 8192], P(None, 'inst')
The draws below stay inside these ranges and needn't reach their ends.
Inputs may be any that keep to these rules, and one draw needn't show every extreme that they name: `routes`: among the 32 pages of each instance no instance is named more than 1 times.
All inputs are finite; a program needn't handle non-finite values.
Results may differ from the reference program's by a relative error of at most 0.015.
Values may be sent and summed in bfloat16 or wider, within the bound.
A program may use at most 64 MiB of HBM per device.

```python
import math
import jax
import jax.numpy as jnp
import numpy as np
from jax import lax

HQ = 64
KVH = 8
HD = 128
D = 8192
Q_DEV = 64
PAGE = 8
CAP = 1
PG_DEV = 32
CTX_DEV = 256
CONTEXT = 16384
SPAN = 4096
PAGES = 2048
HELD = 64
N_INST = 64


def query_base(key):
    return jax.random.normal(jax.random.fold_in(key, 5), (KVH, HD), jnp.float32)


def clipped_normal(key, shape):
    return jnp.clip(1.5 * jax.random.normal(key, shape, jnp.float32), -8.0, 8.0)


def draw_key_cache(key, part):
    key = jax.random.fold_in(key, 11)
    values = clipped_normal(key, (CONTEXT, KVH, HD))
    return values.astype(jnp.bfloat16)


def draw_span_keys(key, part):
    key = jax.random.fold_in(key, 23)
    values = clipped_normal(key, (SPAN, KVH, HD))
    return values.astype(jnp.bfloat16)


def draw_query(key, part):
    key = jax.random.fold_in(key, 37)
    values = clipped_normal(key, (SPAN, HQ, HD))
    return values.astype(jnp.bfloat16)


def draw_decode_query(key, part):
    shared = jnp.repeat(query_base(key), HQ // KVH, axis=0)
    key = jax.random.fold_in(key, 41)
    noise = jax.random.normal(key, (HQ, HD), jnp.float32)
    values = jnp.clip(1.5 * shared + 0.5 * noise, -8.0, 8.0)
    return values.astype(jnp.bfloat16)


def draw_new_key(key, part):
    shared = query_base(key)
    key = jax.random.fold_in(key, 53)
    noise = jax.random.normal(key, (KVH, HD), jnp.float32)
    factor = 2.0 * (16.0 / HD) ** 0.5
    return jnp.clip(factor * shared + 0.3 * noise, -8.0, 8.0).astype(jnp.bfloat16)


def with_ends(entries, rng, least, high):
    place = [jax.random.randint(jax.random.fold_in(rng, axis), (), 0, length) for axis, length in enumerate(entries.shape)]
    longest = entries.shape.index(max(entries.shape))
    beside = place[:longest] + [(place[longest] + 1) % entries.shape[longest]] + place[longest + 1:]
    return entries.at[tuple(place)].set(least).at[tuple(beside)].set(high)


def levels(key, dims, cuts, least, high):
    def one(position, blocks):
        steps = jax.random.uniform(jax.random.fold_in(jax.random.fold_in(key, 6), position), (blocks,), jnp.float32, least / len(cuts), high / len(cuts))
        return jnp.repeat(jnp.exp(steps), dims[position] // blocks).reshape((-1,) + (1,) * (len(dims) - position - 1))

    factor_of = one(*cuts[0])
    for cut in cuts[1:]:
        factor_of = factor_of * one(*cut)
    return factor_of


def shared_out(key, own, number, rows, count, top, limit, skew):
    sequence = jax.random.permutation(key, count)
    crowded, common = load_shares(count, rows * top, limit, skew, True), load_shares(count, rows * top, limit, skew, False)
    places = jnp.arange(count)

    def named(lengths, rotation):
        used = int((lengths > 0).sum())
        fixed = max(1, used // 4)
        moved = fixed + (places - fixed + rotation * (used - fixed)) % max(1, count - fixed)
        return jnp.zeros((count,), jnp.int32).at[sequence[jnp.where(places < fixed, places, moved)]].set(jnp.asarray(lengths, jnp.int32))

    lengths = jnp.where(number % 4 == 0, named(crowded, number // 4), named(common, number - number // 4 - 1))
    mixed = jax.random.permutation(jax.random.fold_in(own, 3), count)
    source_of, taker = mixed[0:count // 2 * 2:2], mixed[1:count // 2 * 2:2]
    slack = jnp.minimum(lengths[source_of] - 1, limit - lengths[taker]) // 2
    slack = jnp.where((source_of == sequence[0]) | (taker == sequence[0]) | (lengths[taker] == 0), 0, jnp.maximum(slack, 0))
    moved = jax.random.randint(jax.random.fold_in(own, 4), (count // 2,), 0, 1 << 20) % (slack + 1)
    lengths = lengths.at[source_of].add(-moved).at[taker].add(moved)
    labels = jnp.searchsorted(jnp.cumsum(lengths), jnp.arange(rows * top), side="right").astype(jnp.int32)
    grid = labels.reshape(top, rows).T
    grid = grid[jax.random.permutation(jax.random.fold_in(own, 1), rows)]
    rotation = jax.random.randint(jax.random.fold_in(own, 2), (rows, 1), 0, top)
    return jnp.take_along_axis(grid, (jnp.arange(top)[None, :] + rotation) % top, axis=1)


def load_shares(amount, total, limit, slope, full):
    portions = [(1 << 20) // math.isqrt(rank ** slope) + 1 for rank in range(1, amount + 1)]
    largest = limit if full else min(limit, max(-(-total // amount), total * portions[0] // sum(portions)))
    least = 1 if total - largest >= amount - 1 else 0
    counts, surplus = [largest] + [least] * (amount - 1), total - largest - least * (amount - 1)
    while surplus > 0:
        candidates = [i for i in range(1, amount) if counts[i] < largest] or [i for i in range(1, amount) if counts[i] < limit]
        mass, remaining = sum([portions[i] for i in candidates]), surplus
        for i in candidates:
            extra = min(limit - counts[i], max(1, remaining * portions[i] // mass), surplus)
            counts[i] = counts[i] + extra
            surplus = surplus - extra
    return np.array(counts)


def scatter_about(own_key, shape, deviation, most, cuts=(), kind=jnp.bfloat16):
    values = jax.random.normal(own_key, shape, jnp.float32) * deviation
    if len(cuts) > 0:
        values = levels(own_key, shape, cuts, -0.22, 0.18) * values
    return jnp.clip(values, min=-most, max=most).astype(kind)


def setup_inputs(seed: int = 0) -> dict:
    seeds = jax.random.split(jax.random.key(seed), 12)
    query = draw_query(jax.random.fold_in(seeds[11], 71), 0)
    key_cache = draw_key_cache(jax.random.fold_in(seeds[11], 71), 0)
    value_cache = scatter_about(seeds[2], (CONTEXT, KVH, HD), 1.0, 6.0, ((0, 64), (1, 8)))
    span_keys = draw_span_keys(jax.random.fold_in(seeds[11], 71), 0)
    span_values = scatter_about(seeds[4], (SPAN, KVH, HD), 1.0, 6.0, ((0, 64), (1, 8)))
    live_pages = with_ends(jax.random.randint(seeds[5], (N_INST,), PG_DEV - PG_DEV // 4, PG_DEV + 1), jax.random.fold_in(seeds[5], 1), PG_DEV - PG_DEV // 4, PG_DEV).astype(jnp.int32)
    routes_keys = jax.random.split(jax.random.fold_in(seeds[6], 1), PAGES // PG_DEV)
    routes_turns = jax.random.permutation(jax.random.fold_in(seeds[6], 3), PAGES // PG_DEV)
    routes = jax.vmap(lambda own, number: shared_out(jax.random.fold_in(seeds[6], 2), own, number, PG_DEV, N_INST, 1, CAP, 2))(routes_keys, routes_turns).reshape((PAGES, 1))
    decode_query = draw_decode_query(jax.random.fold_in(seeds[11], 71), 0)
    new_key = draw_new_key(jax.random.fold_in(seeds[11], 71), 0)
    new_value = scatter_about(seeds[9], (KVH, HD), 1.0, 6.0, ((0, 8),))
    w_out = scatter_about(seeds[10], (HQ * HD, D), (HQ * HD) ** -0.5, 0.0625, ((0, 8), (1, 64)))
    return dict(query=query, key_cache=key_cache, value_cache=value_cache, span_keys=span_keys, span_values=span_values, live_pages=live_pages, routes=routes, decode_query=decode_query, new_key=new_key, new_value=new_value, w_out=w_out)


def attend(scores, value_rows, form):
    peak = lax.optimization_barrier(jnp.max(scores, axis=-1, keepdims=True))
    weights = jnp.exp(scores - peak)
    weight_sum = lax.optimization_barrier(jnp.sum(weights, axis=-1))
    rounded = weights.astype(jnp.bfloat16).astype(jnp.float32)
    mixed = jnp.einsum(form, rounded, value_rows)
    return (mixed / weight_sum[..., None]).astype(jnp.bfloat16)

def reference(query, key_cache, value_cache, span_keys, span_values, live_pages, routes, decode_query, new_key, new_value, w_out):
    groups = HQ // KVH
    score_scale = 1.0 / math.sqrt(HD)
    key_rows = jnp.concatenate([key_cache, span_keys], 0).astype(jnp.float32)
    value_rows = jnp.concatenate([value_cache, span_values], 0).astype(jnp.float32)
    positions = jnp.arange(CONTEXT + SPAN, dtype=jnp.int32)
    owner = jnp.minimum(positions // CTX_DEV, N_INST - 1).astype(jnp.int32)
    is_cache = positions < CONTEXT
    cache_alive = positions % CTX_DEV // PAGE < live_pages[owner]
    span_index = positions - CONTEXT
    blocks = query.reshape(N_INST, Q_DEV, KVH, groups, HD)
    starts = jnp.arange(N_INST, dtype=jnp.int32) * Q_DEV

    def one_block(operands):
        block, first_row = operands
        rows = first_row + jnp.arange(Q_DEV, dtype=jnp.int32)
        allowed = jnp.where(is_cache[None, :], cache_alive[None, :], span_index[None, :] <= rows[:, None])
        scores = jnp.einsum('qkgd,ckd->qkgc', block.astype(jnp.float32), key_rows) * score_scale
        scores = jnp.where(allowed[:, None, None, :], scores, -jnp.inf)
        return attend(scores, value_rows, 'qkgc,ckd->qkgd')
    span_out = lax.map(one_block, (blocks, starts)).reshape(SPAN, HQ, HD)
    route_grid = routes.reshape(N_INST, PG_DEV)
    page_order = jnp.arange(PG_DEV, dtype=jnp.int32)
    same_holder = route_grid[:, :, None] == route_grid[:, None, :]
    earlier = page_order[None, :] < page_order[:, None]
    page_rank = lax.optimization_barrier(jnp.sum((same_holder & earlier[None]).astype(jnp.int32), axis=2))
    sources = jnp.arange(N_INST, dtype=jnp.int32)[:, None]
    target = route_grid * HELD + sources * CAP + page_rank
    in_use = (page_order[None, :] < live_pages[:, None]).reshape(-1)
    target = target.reshape(-1)
    page_keys = key_cache.reshape(PAGES, PAGE, KVH, HD)
    page_values = value_cache.reshape(PAGES, PAGE, KVH, HD)
    held_keys = jnp.zeros((N_INST * HELD, PAGE, KVH, HD), key_cache.dtype).at[target].set(jnp.where(in_use[:, None, None, None], page_keys, 0))
    held_values = jnp.zeros((N_INST * HELD, PAGE, KVH, HD), value_cache.dtype).at[target].set(jnp.where(in_use[:, None, None, None], page_values, 0))
    page_ids = jnp.arange(PAGES, dtype=jnp.int32)
    held_pages = jnp.full((N_INST * HELD,), -1, jnp.int32).at[target].set(jnp.where(in_use, page_ids, -1))
    step_query = decode_query.reshape(KVH, groups, HD).astype(jnp.float32)
    all_keys = jnp.concatenate([key_rows, new_key[None].astype(jnp.float32)], 0)
    all_values = jnp.concatenate([value_rows, new_value[None].astype(jnp.float32)], 0)
    decode_allowed = jnp.concatenate([jnp.where(is_cache, cache_alive, True), jnp.ones((1,), bool)])
    dscores = jnp.einsum('kgd,ckd->kgc', step_query, all_keys) * score_scale
    dscores = jnp.where(decode_allowed[None, None, :], dscores, -jnp.inf)
    attended = attend(dscores, all_values, 'kgc,ckd->kgd').reshape(1, HQ * HD)
    decoded = jnp.dot(attended, w_out, preferred_element_type=jnp.float32).astype(jnp.bfloat16)
    return (span_out, held_keys, held_values, held_pages, decoded)
```

```python
import functools
import math

import jax
import jax.numpy as jnp
from jax import lax
from jax.experimental import pallas as pl
from jax.experimental.pallas import tpu as pltpu
from jax.sharding import PartitionSpec as P

f32, bf16, i32 = jnp.float32, jnp.bfloat16, jnp.int32
MESH = pl.DeviceIdType.MESH
NEG = -1e30
NX, NY = 4, 8
HD, G = 128, 8
Q_DEV, CTX, PAGE, PG = 64, 256, 8, 32
R = Q_DEV * G
KROWS = CTX + Q_DEV + 16
VROWS = HD + 32
N = 2 * (CTX + Q_DEV)
SCALE = math.log2(math.e) / math.sqrt(HD)


def nt(a, b):
    return lax.dot_general(a, b, (((1,), (1,)), ((), ())), preferred_element_type=f32)


def nn(a, b):
    return lax.dot_general(a, b, (((1,), (0,)), ((), ())), preferred_element_type=f32)


def iota(shape, dim):
    return lax.broadcasted_iota(i32, shape, dim)


def unit(f):
    turn, group = (f - 1) % 3, (f - 1) // 3
    last = f >= 25
    block = jnp.where(turn == 0, 1, jnp.where(turn == 1, 2, 3))
    block = jnp.where(f == 3, 0, jnp.where(last, jnp.where(f == 25, 3, 0), block))
    k = jnp.where(turn == 2, group - 1, group)
    k = jnp.where(f == 3, 1, jnp.where(last, jnp.where(f == 25, 7, f - 24), k))
    own_first = f == 0
    return jnp.where(own_first, 0, block), jnp.where(own_first, 0, k)


def merge(parts):
    o, m, l = parts[:, 0:8], parts[:, 8:16], parts[:, 16:24]
    peak = jnp.max(m, axis=0)
    w = jnp.exp2(m - peak[None])
    return jnp.sum(w * o, axis=0), peak, jnp.sum(w * l, axis=0)


def kernel(
    nz,
    q_in, kc_in, vc_in, sk_in, sv_in, w_in, live_in, routes_in, dq_in, nk_in, nv_in,
    out, hk_out, hv_out, ids_out, dec_out,
    Kb, Vb, Db, Qb, vtmp, svb, wb, acc, m, l, Sa, Sb, Pa, Pb, al_a, al_b, mn_a, mn_b,
    Os, Or, Ts, Tr, PKs, PKr, Is, Ir, DX, Zb, ostage,
    lsem, sK, sV, sD, rK, rV, rD, sSV, rSV, sQ, rQ, sO, rO, sT, rT, sP, rP, sI, rI, sX, rX,
    sZ, rZ,
):
    me = lax.axis_index("inst")
    z = lax.axis_index("tp")
    c = me % 2
    x = (me // 2) % NX
    y = me // (2 * NX)

    def inst(yy, xx, cc):
        return (yy * NX + xx) * 2 + cc

    def ymod(v):
        return (v + 2 * NY) % NY

    sib = inst(y, x, 1 - c)
    up = inst(ymod(y + 1), x, c)
    down = inst(ymod(y - 1), x, c)
    xs = [x, (x + NX - 1) % NX, (x + 1) % NX, (x + 2) % NX]
    xpeer = [inst(y, v, c) for v in xs]
    mine = y * 2 + c

    def xblock(b):
        return (x + jnp.where(b == 1, NX - 1, jnp.where(b == 2, 1, jnp.where(b == 3, 2, 0)))) % NX

    def chip(k):
        return ymod(y + jnp.where(k == 7, 4, jnp.where(k % 2 == 1, -((k + 1) // 2), k // 2)))

    def remote(src, dst, ss, rs, to, zz=None):
        return pltpu.make_async_remote_copy(
            src_ref=src, dst_ref=dst, send_sem=ss, recv_sem=rs,
            device_id=(to, z if zz is None else zz), device_id_type=MESH,
        )

    loads = [
        pltpu.make_async_copy(kc_in, Kb.at[mine, 0:CTX], lsem.at[0]),
        pltpu.make_async_copy(sk_in, Kb.at[mine, CTX:CTX + Q_DEV], lsem.at[1]),
        pltpu.make_async_copy(sv_in, svb.at[c], lsem.at[2]),
        pltpu.make_async_copy(q_in, Qb.at[x], lsem.at[3]),
        pltpu.make_async_copy(vc_in, vtmp, lsem.at[4]),
        pltpu.make_async_copy(w_in, wb, lsem.at[5]),
    ]
    for load in loads:
        load.start()

    barrier = pltpu.get_barrier_semaphore()
    zpeers = [(z + j) % nz for j in range(1, nz)]
    for to in (sib, up, down, xpeer[1], xpeer[2], xpeer[3]):
        pl.semaphore_signal(barrier, inc=1, device_id=(to, z), device_id_type=MESH)
    for zz in zpeers:
        pl.semaphore_signal(barrier, inc=1, device_id=(me, zz), device_id_type=MESH)

    live_rows = live_in[0] * PAGE
    wide = iota((PG, CTX), 1) // PAGE == iota((PG, CTX), 0)
    per_token = jnp.sum(
        jnp.where(wide, routes_in[...].astype(f32), 0.0), axis=0, keepdims=True
    )
    row = iota((16, HD), 0)
    info = jnp.where(row == 0, live_rows.astype(f32), 0.0)
    info = jnp.where(row == 1, per_token[:, 0:HD], info)
    info = jnp.where(row == 2, per_token[:, HD:2 * HD], info)
    Kb[mine, CTX + Q_DEV:KROWS, :] = info.astype(bf16)
    for v in range(4):
        m[v] = jnp.full((8, R), NEG, f32)
        l[v] = jnp.zeros((8, R), f32)
        acc[v] = jnp.zeros((HD, R), f32)

    loads[0].wait()
    loads[1].wait()
    loads[2].wait()
    loads[3].wait()
    pl.semaphore_wait(barrier, 6 + nz - 1)

    def piece(kind, yy, way):
        buf, ss, rs = ((Kb, sK, rK), (Vb, sV, rV), (Db, sD, rD))[kind]
        s = yy * 2 + c
        return remote(buf.at[s], buf.at[s], ss.at[way, yy], rs.at[s], (up, down, sib)[way])

    def arrived(kind, s):
        buf, ss, rs = ((Kb, sK, rK), (Vb, sV, rV), (Db, sD, rD))[kind]
        remote(buf.at[s], buf.at[s], ss.at[0, 0], rs.at[s], sib).wait_recv()

    def qcopy(j):
        return remote(Qb.at[x], Qb.at[x], sQ.at[j], rQ.at[x], xpeer[j])

    span_copy = remote(svb.at[c], svb.at[c], sSV, rSV, sib)
    piece(0, y, 2).start()
    span_copy.start()
    piece(0, y, 0).start()
    piece(0, y, 1).start()
    qcopy(1).start()
    qcopy(2).start()

    loads[4].wait()
    Vb[mine, 0:HD, :] = vtmp[...].astype(f32).T.astype(bf16)
    remote(svb.at[1 - c], svb.at[1 - c], sSV, rSV, sib).wait_recv()
    both = jnp.concatenate([svb[0], svb[1]], axis=0).astype(f32).T
    half = jnp.where(c == 0, both[0:64], both[64:128])
    Vb[mine, HD:VROWS, :] = jnp.concatenate([half[0:32], half[32:64]], axis=1).astype(bf16)
    piece(1, y, 2).start()
    piece(1, y, 0).start()
    piece(1, y, 1).start()
    qcopy(3).start()

    dq = dq_in[...]
    s_cache = nt(dq, Kb[mine, 0:CTX, :]) * SCALE
    s_cache = jnp.where(iota((G, CTX), 1) < live_rows, s_cache, NEG)
    s_span = nt(dq, Kb[mine, CTX:CTX + Q_DEV, :]) * SCALE
    peak = jnp.maximum(
        jnp.max(s_cache, axis=1, keepdims=True), jnp.max(s_span, axis=1, keepdims=True)
    )
    p_cache, p_span = jnp.exp2(s_cache - peak), jnp.exp2(s_span - peak)
    weight = jnp.sum(p_cache, axis=1, keepdims=True) + jnp.sum(p_span, axis=1, keepdims=True)
    mixed = nt(p_cache.astype(bf16), Vb[mine, 0:HD, :]) + nn(p_span.astype(bf16), svb[c])
    Db[mine, 0:8, :] = mixed
    Db[mine, 8:16, :] = jnp.broadcast_to(peak, (8, HD))
    Db[mine, 16:24, :] = jnp.broadcast_to(weight, (8, HD))
    piece(2, y, 2).start()
    piece(2, y, 0).start()
    piece(2, y, 1).start()

    def scores(f, S, al, mn):
        block, k = unit(f)
        xq, yk = xblock(block), chip(k)
        q = Qb[xq]
        top = None
        for cc in range(2):
            s = yk * 2 + cc
            limit = Kb[s, CTX + Q_DEV:KROWS, :].astype(f32)[0:1, :]
            for h in range(2):
                sc = nt(Kb[s, h * HD:(h + 1) * HD, :], q)
                ok = (iota((HD, HD), 0) + h * HD).astype(f32) < limit
                sc = jnp.concatenate(
                    [jnp.where(ok, sc[:, t * HD:(t + 1) * HD], NEG) for t in range(R // HD)],
                    axis=1,
                )
                at = (cc * 2 + h) * HD
                S[at:at + HD, :] = sc
                best = jnp.max(sc.reshape(HD // 8, 8, R), axis=0)
                top = best if top is None else jnp.maximum(top, best)
                yield
        keys = jnp.concatenate(
            [Kb[yk * 2, CTX:CTX + Q_DEV, :], Kb[yk * 2 + 1, CTX:CTX + Q_DEV, :]], axis=0
        )
        sc = nt(keys, q)
        ahead = (inst(y, xq, c) - inst(yk, x, 0)) * Q_DEV
        sc = jnp.where(iota((HD, R), 0) <= iota((HD, R), 1) // G + ahead, sc, NEG)
        S[4 * HD:5 * HD, :] = sc
        top = jnp.maximum(top, jnp.max(sc.reshape(HD // 8, 8, R), axis=0))
        yield
        old = m[xq]
        new = jnp.maximum(old, jnp.max(top, axis=0, keepdims=True) * SCALE)
        al[...] = jnp.exp2(old - new)
        mn[...] = new
        m[xq] = new

    def weights(f, S, Pw, al, mn):
        block, _ = unit(f)
        xq = xblock(block)
        shrink, peak = al[...], mn[0:1, :]
        total = None
        for j in range(5):
            p = jnp.exp2(S[j * HD:(j + 1) * HD, :] * SCALE - peak)
            Pw[j * HD:(j + 1) * HD, :] = p.astype(bf16)
            part = jnp.sum(p.reshape(HD // 8, 8, R), axis=0)
            total = part if total is None else total + part
            yield
        l[xq] = l[xq] * shrink + total

    def values(f, Pw, al):
        block, k = unit(f)
        xq, yk = xblock(block), chip(k)
        shrink = al[0:1, :]
        s0, s1 = yk * 2, yk * 2 + 1
        span = jnp.concatenate(
            [Vb[s, HD:VROWS, t * HD:(t + 1) * HD] for s in (s0, s1) for t in range(2)], axis=0
        )
        vt = jnp.concatenate([Vb[s0, 0:HD, :], Vb[s1, 0:HD, :], span], axis=1)
        mix = nn(vt, Pw[...])
        for _ in range(4):
            yield
        acc[xq] = acc[xq] * shrink + mix

    def together(*stages):
        stages = list(stages)
        while stages:
            stages = [s for s in stages if next(s, stages) is None]

    def wait_chip(kind, k):
        arrived(kind, chip(k) * 2 + 1 - c)

    def pass_keys(d):
        yu, yd = ymod(y - d), ymod(y + d)
        arrived(0, yu * 2 + c)

        @pl.when(d < 4)
        def _():
            piece(0, yu, 0).start()

        piece(0, yu, 2).start()

        @pl.when(d < 4)
        def _():
            arrived(0, yd * 2 + c)

            @pl.when(d < 3)
            def _():
                piece(0, yd, 1).start()

            piece(0, yd, 2).start()

    def pass_values(d):
        yu, yd = ymod(y - d), ymod(y + d)
        for kind in (1, 2):
            @pl.when(d < 4)
            def _():
                arrived(kind, yu * 2 + c)

                @pl.when(d < 3)
                def _():
                    piece(kind, yu, 0).start()

                piece(kind, yu, 2).start()

            arrived(kind, yd * 2 + c)

            @pl.when(d < 4)
            def _():
                piece(kind, yd, 1).start()

            piece(kind, yd, 2).start()

    def pages(k):
        yk = chip(k)
        r, tok = iota((32, CTX), 0), iota((32, CTX), 1)
        to = (y * 2 * NX + (r // 8) * 2 + c).astype(f32)
        got_k, got_v = [], []
        for cc in range(2):
            s = yk * 2 + cc
            meta = Kb[s, CTX + Q_DEV:KROWS, :].astype(f32)
            limit = jnp.concatenate([meta[0:1, :]] * 2, axis=1)
            route = jnp.concatenate([meta[1:2, :], meta[2:3, :]], axis=1)
            hit = (route == to) & (tok % 8 == r % 8) & (tok.astype(f32) < limit)
            pick = jnp.where(hit, 1.0, 0.0)
            one = pick.astype(bf16)
            got_k.append(nn(one, Kb[s, 0:CTX, :]))
            got_v.append(nt(one, Vb[s, 0:HD, :]))
            number = inst(yk, x, cc) * PG + tok // PAGE + 1
            found = jnp.sum(jnp.where(hit, number, 0).astype(f32), axis=1, keepdims=True) - 1.0
            for v in range(NX):
                Is[v, pl.ds(s, 1), :] = jnp.broadcast_to(
                    found[v * 8:v * 8 + 1, :], (1, HD)
                ).astype(i32)
        for v in range(NX):
            for half, got in enumerate((got_k, got_v)):
                rows = jnp.concatenate([g[v * 8:v * 8 + 8, :] for g in got], axis=0)
                PKs[v, half, yk] = rows.astype(bf16)

    def send_pages():
        for j in (1, 2, 3):
            remote(PKs.at[xs[j]], PKr.at[x], sP.at[j], rP.at[x], xpeer[j]).start()
            remote(Is.at[xs[j]], Ir.at[x], sI.at[j], rI.at[x], xpeer[j]).start()

    def out_copies(j):
        return (
            remote(Os.at[xs[j]], Or.at[x], sO.at[j], rO.at[x], xpeer[j]),
            remote(Ts.at[xs[j]], Tr.at[x], sT.at[j], rT.at[x], xpeer[j]),
        )

    def send_out(j):
        v = xs[j]
        Os[v] = acc[v].astype(bf16)
        total = jnp.sum(l[v], axis=0, keepdims=True)
        Ts[v] = jnp.where(iota((8, R), 0) == 0, m[v], total)
        for copy in out_copies(j):
            copy.start()

    def decode_column():
        for k in range(8):
            arrived(2, chip(k) * 2 + 1 - c)
        o, peak, weight = merge(Db[...])
        DX[x, 0:8, :] = o
        DX[x, 8:16, :] = peak
        DX[x, 16:24, :] = weight
        for j in (1, 2, 3):
            remote(DX.at[x], DX.at[x], sX.at[j], rX.at[x], xpeer[j]).start()

    def decode_project():
        for j in (1, 2, 3):
            remote(DX.at[xs[j]], DX.at[xs[j]], sX.at[j], rX.at[xs[j]], xpeer[j]).wait_recv()
        o, peak, weight = merge(DX[...])
        own = jnp.sum(dq.astype(f32) * nk_in[...].astype(f32), axis=1, keepdims=True) * SCALE
        last = jnp.maximum(peak, own)
        shrink, extra = jnp.exp2(peak - last), jnp.exp2(own - last)
        weight = weight * shrink + extra
        o = o * shrink + extra.astype(bf16).astype(f32) * nv_in[...].astype(f32)
        attended = (o / weight).astype(bf16).astype(f32)
        head = iota((G, HD), 0)
        wide = jnp.concatenate(
            [jnp.where(head == h, attended, 0.0) for h in range(G)], axis=1
        ).astype(bf16)
        loads[5].wait()
        Zb[z] = nn(wide, wb[...])
        for j, zz in enumerate(zpeers):
            remote(Zb.at[z], Zb.at[z], sZ.at[j], rZ.at[z], me, zz).start()

    def hooks(f):
        @pl.when((f % 6 == 1) & (f < 20))
        def _():
            pass_keys((f + 5) // 6)

        @pl.when((f % 6 == 3) & (f < 22))
        def _():
            pass_values((f + 3) // 6)

        @pl.when(f == 1)
        def _():
            remote(Qb.at[xs[2]], Qb.at[xs[2]], sQ.at[2], rQ.at[xs[2]], xpeer[2]).wait_recv()

        @pl.when(f == 5)
        def _():
            remote(Qb.at[xs[3]], Qb.at[xs[3]], sQ.at[3], rQ.at[xs[3]], xpeer[3]).wait_recv()

        @pl.when((f == 2) | ((f % 3 == 0) & (f >= 6) & (f <= 21)))
        def _():
            wait_chip(0, jnp.where(f == 2, 1, f // 3))

        @pl.when((f == 4) | ((f % 3 == 2) & (f >= 8) & (f <= 23)))
        def _():
            wait_chip(1, jnp.where(f == 4, 1, (f - 2) // 3))

        @pl.when((f % 3 == 2) & (f <= 23))
        def _():
            pages((f - 2) // 3)

        @pl.when(f == 23)
        def _():
            send_pages()

        for j, at in ((1, 24), (2, 25), (3, 27)):
            @pl.when(f == at)
            def _():
                send_out(j)

        @pl.when(f == 24)
        def _():
            decode_column()

        @pl.when(f == 28)
        def _():
            decode_project()

    zero = jnp.int32(0)
    arrived(0, sib % 2 + y * 2)
    together(scores(zero, Sa, al_a, mn_a))
    remote(Qb.at[xs[1]], Qb.at[xs[1]], sQ.at[1], rQ.at[xs[1]], xpeer[1]).wait_recv()
    together(scores(zero + 1, Sb, al_b, mn_b), weights(zero, Sa, Pa, al_a, mn_a))
    arrived(1, sib % 2 + y * 2)

    def body(f, Sc, Sn, Pc, Pp, alc, alo, mnc, mno):
        hooks(f)
        together(
            values(f - 1, Pp, alo), weights(f, Sc, Pc, alc, mnc), scores(f + 1, Sn, alo, mno)
        )

    def pair(i, carry):
        f = 1 + 2 * i
        body(f, Sb, Sa, Pb, Pa, al_b, al_a, mn_b, mn_a)
        body(f + 1, Sa, Sb, Pa, Pb, al_a, al_b, mn_a, mn_b)
        return carry

    lax.fori_loop(0, 15, pair, 0)
    last = zero + 31
    together(values(last - 1, Pa, al_a), weights(last, Sb, Pb, al_b, mn_b))
    together(values(last, Pb, al_b))

    for j in (1, 2, 3):
        v = xs[j]
        remote(PKs.at[v], PKr.at[v], sP.at[j], rP.at[v], xpeer[j]).wait_recv()
        remote(Is.at[v], Ir.at[v], sI.at[j], rI.at[v], xpeer[j]).wait_recv()
    PKr[x] = PKs[x]
    Ir[x] = Is[x]
    stores = [
        pltpu.make_async_copy(PKr.at[v, half], ref.at[:, v], lsem.at[8 + half * NX + v])
        for half, ref in enumerate((hk_out, hv_out)) for v in range(NX)
    ]
    stores.append(pltpu.make_async_copy(Ir, ids_out, lsem.at[6]))
    for store in stores:
        store.start()

    for j, zz in enumerate(zpeers):
        remote(Zb.at[zz], Zb.at[zz], sZ.at[j], rZ.at[zz], me, zz).wait_recv()
    total = Zb[0]
    for v in range(1, nz):
        total = total + Zb[v]
    dec_out[...] = jnp.sum(total, axis=0, keepdims=True).astype(bf16)

    for j in (1, 2, 3):
        v = xs[j]
        remote(Os.at[v], Or.at[v], sO.at[j], rO.at[v], xpeer[j]).wait_recv()
        remote(Ts.at[v], Tr.at[v], sT.at[j], rT.at[v], xpeer[j]).wait_recv()
    peaks = [m[x][0:1, :]] + [Tr[xs[j], 0:1, :] for j in (1, 2, 3)]
    sums = [jnp.sum(l[x], axis=0, keepdims=True)] + [Tr[xs[j], 1:2, :] for j in (1, 2, 3)]
    peak = functools.reduce(jnp.maximum, peaks)
    shares = [jnp.exp2(p - peak) for p in peaks]
    whole = sum(w * s for w, s in zip(shares, sums))
    shares = [w / whole for w in shares]
    mix = acc[x] * shares[0]
    for j in (1, 2, 3):
        mix = mix + Or[xs[j]].astype(f32) * shares[j]
    ostage[...] = mix.T.astype(bf16)
    done = pltpu.make_async_copy(ostage, out, lsem.at[7])
    done.start()

    for kind in range(3):
        for d in range(4):
            if kind == 0 or d < 3:
                piece(kind, ymod(y - d), 0).wait_send()
            if d < 3 or kind > 0:
                piece(kind, ymod(y + d), 1).wait_send()
        for yy in range(NY):
            piece(kind, yy, 2).wait_send()
    span_copy.wait_send()
    for j in (1, 2, 3):
        qcopy(j).wait_send()
        for copy in out_copies(j):
            copy.wait_send()
        remote(PKs.at[xs[j]], PKr.at[x], sP.at[j], rP.at[x], xpeer[j]).wait_send()
        remote(Is.at[xs[j]], Ir.at[x], sI.at[j], rI.at[x], xpeer[j]).wait_send()
        remote(DX.at[x], DX.at[x], sX.at[j], rX.at[x], xpeer[j]).wait_send()
    for j, zz in enumerate(zpeers):
        remote(Zb.at[z], Zb.at[z], sZ.at[j], rZ.at[z], me, zz).wait_send()
    for store in stores:
        store.wait()
    done.wait()


def local(
    nz,
    query, key_cache, value_cache, span_keys, span_values, live_pages, routes,
    decode_query, new_key, new_value, w_out,
):
    hbm = pl.BlockSpec(memory_space=pl.ANY)
    vmem = pl.BlockSpec(memory_space=pltpu.VMEM)
    smem = pl.BlockSpec(memory_space=pltpu.SMEM)
    V, D = pltpu.VMEM, pltpu.SemaphoreType.DMA
    out, hk, hv, ids, decoded = pl.pallas_call(
        functools.partial(kernel, nz),
        out_shape=(
            jax.ShapeDtypeStruct((R, HD), bf16),
            jax.ShapeDtypeStruct((NY, NX, 16, HD), bf16),
            jax.ShapeDtypeStruct((NY, NX, 16, HD), bf16),
            jax.ShapeDtypeStruct((NX, 16, HD), i32),
            jax.ShapeDtypeStruct((1, HD), bf16),
        ),
        in_specs=[hbm] * 6 + [smem] + [vmem] * 4,
        out_specs=(hbm, hbm, hbm, hbm, vmem),
        scratch_shapes=[
            V((2 * NY, KROWS, HD), bf16), V((2 * NY, VROWS, CTX), bf16), V((2 * NY, 24, HD), f32),
            V((NX, R, HD), bf16), V((CTX, HD), bf16), V((2, Q_DEV, HD), bf16),
            V((HD * G, HD), bf16),
            V((NX, HD, R), f32), V((NX, 8, R), f32), V((NX, 8, R), f32),
            V((N, R), f32), V((N, R), f32), V((N, R), bf16), V((N, R), bf16),
            V((8, R), f32), V((8, R), f32), V((8, R), f32), V((8, R), f32),
            V((NX, HD, R), bf16), V((NX, HD, R), bf16), V((NX, 8, R), f32), V((NX, 8, R), f32),
            V((NX, 2, NY, 16, HD), bf16), V((NX, 2, NY, 16, HD), bf16),
            V((NX, 16, HD), i32), V((NX, 16, HD), i32),
            V((NX, 24, HD), f32), V((nz, 8, HD), f32), V((R, HD), bf16),
            D((16,)),
            D((3, NY)), D((3, NY)), D((3, NY)), D((2 * NY,)), D((2 * NY,)), D((2 * NY,)),
            D, D,
            D((NX,)), D((NX,)), D((NX,)), D((NX,)), D((NX,)), D((NX,)), D((NX,)), D((NX,)),
            D((NX,)), D((NX,)), D((NX,)), D((NX,)),
            D((nz,)), D((nz,)),
        ],
        compiler_params=pltpu.CompilerParams(
            collective_id=0, has_side_effects=True, vmem_limit_bytes=48 * 2**20
        ),
        cost_estimate=pl.CostEstimate(
            flops=4 * R * 64 * (CTX + Q_DEV) * HD, bytes_accessed=2**20,
            transcendentals=R * 64 * (CTX + Q_DEV),
        ),
        name="attend",
    )(
        query.reshape(R, HD), key_cache.reshape(CTX, HD), value_cache.reshape(CTX, HD),
        span_keys.reshape(Q_DEV, HD), span_values.reshape(Q_DEV, HD), w_out,
        live_pages, routes, decode_query, new_key, new_value,
    )
    held = ids[:, :, 0].reshape(NX, NY, 2).transpose(1, 0, 2).reshape(NX * NY * 2)
    return (
        out.reshape(Q_DEV, G, HD),
        hk.reshape(NX * NY * 2, PAGE, 1, HD),
        hv.reshape(NX * NY * 2, PAGE, 1, HD),
        held,
        decoded,
    )


def solution(mesh):
    return jax.shard_map(
        functools.partial(local, mesh.shape["tp"]),
        mesh=mesh,
        in_specs=(
            P("inst", "tp", None),
            P("inst", "tp", None),
            P("inst", "tp", None),
            P("inst", "tp", None),
            P("inst", "tp", None),
            P("inst"),
            P("inst", None),
            P("tp", None),
            P("tp", None),
            P("tp", None),
            P("tp", "inst"),
        ),
        out_specs=(
            P("inst", "tp", None),
            P("inst", None, "tp", None),
            P("inst", None, "tp", None),
            P("inst"),
            P(None, "inst"),
        ),
        check_vma=False,
    )
```

```python
import functools
import math

import jax
import jax.numpy as jnp
from jax import lax
from jax.experimental import pallas as pl
from jax.experimental.pallas import tpu as pltpu
from jax.sharding import PartitionSpec as P

f32, bf16, i32 = jnp.float32, jnp.bfloat16, jnp.int32
MESH = pl.DeviceIdType.MESH
NEG = -1e30
LIMIT = 60 * 2**20
NX, NY = 4, 8
HD, G = 128, 8
Q_DEV, CTX, PAGE, PG = 64, 256, 8, 32
R = Q_DEV * G
KROWS = CTX + Q_DEV + 16
VROWS = HD + 32
N = 6 * (CTX + Q_DEV)
SCALE = math.log2(math.e) / math.sqrt(HD)


def nt(a, b):
    return lax.dot_general(a, b, (((1,), (1,)), ((), ())), preferred_element_type=f32)


def nn(a, b):
    return lax.dot_general(a, b, (((1,), (0,)), ((), ())), preferred_element_type=f32)


def iota(shape, dim):
    return lax.broadcasted_iota(i32, shape, dim)


NEAR, MID, FAR, LAST = (0, 1, 2), (3, 4), (5, 6), (7,)
UNITS = (
    (1, NEAR), (2, NEAR), (0, NEAR), (1, MID), (2, MID), (3, NEAR), (3, MID), (1, FAR), (2, FAR),
    (3, FAR), (3, LAST), (1, LAST), (2, LAST), (0, MID), (0, FAR + LAST),
)


def merge(parts):
    o, m, l = parts[:, 0:8], parts[:, 8:16, 0:1], parts[:, 8:16, HD // 2:HD // 2 + 1]
    peak = jnp.max(m, axis=0)
    w = jnp.exp2(m - peak[None])
    return jnp.sum(w * o, axis=0), peak, jnp.sum(w * l, axis=0)


def kernel(
    nz,
    q_in, kc_in, vc_in, sk_in, sv_in, w_in, live_hbm, routes_hbm, dq_hbm, nk_hbm, nv_hbm,
    out, hk_out, hv_out, ids_out, dec_out,
    live_in, routes_in, dq_in, nk_in, nv_in, held_stage, dec_stage, Kb, Vb, Db, Qb, vtmp, svb, wb, acc, m, l, Sa, Sb, Pa, Pb, al_a, al_b, mn_a, mn_b,
    Os, Or, Ts, Tr, PKs, PKr, Is, Ir, DX, Zb, ostage,
    lsem, sR, rR, sSV, rSV, sQ, rQ, sO, rO, sT, rT, sP, rP, sI, rI, sX, rX,
    sZ, rZ,
):
    me = lax.axis_index("inst")
    z = lax.axis_index("tp")
    c = me % 2
    x = (me // 2) % NX
    y = me // (2 * NX)

    def inst(yy, xx, cc):
        return (yy * NX + xx) * 2 + cc

    def ymod(v):
        return (v + 2 * NY) % NY

    sib = inst(y, x, 1 - c)
    up = inst(ymod(y + 1), x, c)
    down = inst(ymod(y - 1), x, c)
    xs = [x, (x + NX - 1) % NX, (x + 1) % NX, (x + 2) % NX]
    xpeer = [inst(y, v, c) for v in xs]
    mine = y * 2 + c

    around = [ymod(y + v) for v in range(NY)]

    def chip(k):
        return around[(4 if k == 7 else -((k + 1) // 2) if k % 2 else k // 2) % NY]

    def remote(src, dst, ss, rs, to, zz=None):
        return pltpu.make_async_remote_copy(
            src_ref=src, dst_ref=dst, send_sem=ss, recv_sem=rs,
            device_id=(to, z if zz is None else zz), device_id_type=MESH,
        )

    loads = [
        pltpu.make_async_copy(kc_in, Kb.at[mine, 0:CTX], lsem.at[0]),
        pltpu.make_async_copy(sk_in, Kb.at[mine, CTX:CTX + Q_DEV], lsem.at[1]),
        pltpu.make_async_copy(sv_in, svb.at[c], lsem.at[2]),
        pltpu.make_async_copy(q_in, Qb.at[x], lsem.at[3]),
        pltpu.make_async_copy(vc_in, vtmp, lsem.at[4]),
        pltpu.make_async_copy(w_in, wb, lsem.at[5]),
        pltpu.make_async_copy(live_hbm, live_in, lsem.at[16]),
        pltpu.make_async_copy(routes_hbm, routes_in, lsem.at[17]),
        pltpu.make_async_copy(dq_hbm, dq_in, lsem.at[18]),
        pltpu.make_async_copy(nk_hbm, nk_in, lsem.at[19]),
        pltpu.make_async_copy(nv_hbm, nv_in, lsem.at[20]),
    ]
    for load in loads:
        load.start()

    barrier = pltpu.get_barrier_semaphore()
    zpeers = [(z + j) % nz for j in range(1, nz)]
    for to in (sib, up, down, xpeer[1], xpeer[2], xpeer[3]):
        pl.semaphore_signal(barrier, inc=1, device_id=(to, z), device_id_type=MESH)
    for zz in zpeers:
        pl.semaphore_signal(barrier, inc=1, device_id=(me, zz), device_id_type=MESH)

    loads[6].wait()
    loads[7].wait()
    live_rows = live_in[0:1, 0:1] * PAGE
    wide = iota((PG, CTX), 1) // PAGE == iota((PG, CTX), 0)
    per_token = nn(
        jnp.broadcast_to(routes_in[...].astype(f32), (8, PG)).astype(bf16),
        jnp.where(wide, 1.0, 0.0).astype(bf16),
    )[0:1, :]
    row = iota((16, HD), 0)
    info = jnp.where(row == 0, live_rows.astype(f32), 0.0)
    info = jnp.where(row == 1, per_token[:, 0:HD], info)
    info = jnp.where(row == 2, per_token[:, HD:2 * HD], info)
    Kb[mine, CTX + Q_DEV:KROWS, :] = info.astype(bf16)
    for v in range(4):
        Is[v] = jnp.full((8, HD), -1, i32)
        m[v] = jnp.full((8, R), NEG, f32)
        l[v] = jnp.zeros((8, R), f32)
        acc[v] = jnp.zeros((HD, R), f32)

    loads[0].wait()
    loads[1].wait()
    loads[2].wait()
    loads[3].wait()
    pl.semaphore_wait(barrier, 6 + nz - 1)

    def part(p, s):
        if p < 2:
            return Kb.at[s, 176:KROWS] if p else Kb.at[s, 0:176]
        if p < 4:
            return Vb.at[s, VROWS // 2:VROWS] if p == 3 else Vb.at[s, 0:VROWS // 2]
        return Db.at[s]

    def piece(p, yy, way):
        s = yy * 2 + c
        return remote(part(p, s), part(p, s), sR.at[p, way, yy], rR.at[p, s], (up, down, sib)[way])

    def arrived(p, s):
        remote(part(p, s), part(p, s), sR.at[p, 0, 0], rR.at[p, s], sib).wait_recv()

    def qcopy(j):
        return remote(Qb.at[x], Qb.at[x], sQ.at[j], rQ.at[x], xpeer[j])

    span_copy = remote(svb.at[c], svb.at[c], sSV, rSV, sib)
    def send_own(p):
        for way in (0, 1, 2):
            piece(p, y, way).start()

    span_copy.start()
    send_own(0)
    send_own(1)
    qcopy(1).start()
    qcopy(2).start()
    loads[4].wait()
    Vb[mine, 0:HD, :] = vtmp[...].astype(f32).T.astype(bf16)
    remote(svb.at[1 - c], svb.at[1 - c], sSV, rSV, sib).wait_recv()
    both = jnp.concatenate([svb[0], svb[1]], axis=0).astype(f32).T
    half = jnp.where(c == 0, both[0:64], both[64:128])
    Vb[mine, HD:VROWS, :] = jnp.concatenate([half[0:32], half[32:64]], axis=1).astype(bf16)

    def sent(p):
        for way in (0, 1):
            piece(p, y, way).wait_send()

    sent(0)
    send_own(2)
    sent(1)
    send_own(3)

    loads[8].wait()
    dq = dq_in[...]
    s_cache = nt(dq, Kb[mine, 0:CTX, :]) * SCALE
    s_cache = jnp.where(iota((G, CTX), 1) < live_rows, s_cache, NEG)
    s_span = nt(dq, Kb[mine, CTX:CTX + Q_DEV, :]) * SCALE
    peak = jnp.maximum(
        jnp.max(s_cache, axis=1, keepdims=True), jnp.max(s_span, axis=1, keepdims=True)
    )
    p_cache, p_span = jnp.exp2(s_cache - peak), jnp.exp2(s_span - peak)
    weight = jnp.sum(p_cache, axis=1, keepdims=True) + jnp.sum(p_span, axis=1, keepdims=True)
    mixed = nt(p_cache.astype(bf16), Vb[mine, 0:HD, :]) + nn(p_span.astype(bf16), svb[c])
    Db[mine, 0:8, :] = mixed
    Db[mine, 8:16, :] = jnp.where(iota((8, HD), 1) < HD // 2, peak, weight)

    send_own(4)
    qcopy(1).wait_send()
    qcopy(2).wait_send()
    qcopy(3).start()

    bufs = ((Sa, Pa, al_a, mn_a), (Sb, Pb, al_b, mn_b))

    def scores(f):
        block, chips = UNITS[f]
        S, _, al, mn = bufs[f % 2]
        xq, chips = xs[block], [chip(k) for k in chips]
        q = Qb[xq]
        top, at = None, 0
        for yk in chips:
            for cc in range(2):
                s = yk * 2 + cc
                limit = Kb[s, CTX + Q_DEV:KROWS, :].astype(f32)[0:1, :]
                sc = nt(Kb[s, 0:CTX, :], q)
                ok = iota((CTX, HD), 0).astype(f32) < limit
                sc = jnp.concatenate(
                    [jnp.where(ok, sc[:, t * HD:(t + 1) * HD], NEG) for t in range(R // HD)],
                    axis=1,
                )
                S[at:at + CTX, :] = sc
                at += CTX
                best = jnp.max(sc.reshape(CTX // 8, 8, R), axis=0)
                top = best if top is None else jnp.maximum(top, best)
                yield
        for yk in chips:
            keys = jnp.concatenate(
                [Kb[yk * 2, CTX:CTX + Q_DEV, :], Kb[yk * 2 + 1, CTX:CTX + Q_DEV, :]], axis=0
            )
            sc = nt(keys, q)
            ahead = (inst(y, xq, c) - inst(yk, x, 0)) * Q_DEV
            sc = jnp.where(iota((HD, R), 0) <= iota((HD, R), 1) // G + ahead, sc, NEG)
            S[at:at + HD, :] = sc
            at += HD
            top = jnp.maximum(top, jnp.max(sc.reshape(HD // 8, 8, R), axis=0))
        yield
        old = m[xq]
        new = jnp.maximum(old, jnp.max(top, axis=0, keepdims=True) * SCALE)
        al[...] = jnp.exp2(old - new)
        mn[...] = new
        m[xq] = new

    def weights(f):
        block, chips = UNITS[f]
        S, Pw, al, mn = bufs[f % 2]
        xq = xs[block]
        shrink, peak = al[...], mn[0:1, :]
        total = None
        rows = len(chips) * 2 * (CTX + Q_DEV)
        for at in range(0, rows, CTX):
            n = min(CTX, rows - at)
            p = jnp.exp2(S[at:at + n, :] * SCALE - peak)
            Pw[at:at + n, :] = p.astype(bf16)
            part = jnp.sum(p.reshape(n // 8, 8, R), axis=0)
            total = part if total is None else total + part
            yield
        l[xq] = l[xq] * shrink + total

    def values(f):
        block, chips = UNITS[f]
        _, Pw, al, _ = bufs[f % 2]
        xq, chips = xs[block], [chip(k) for k in chips]
        shrink = al[0:1, :]
        cached = [Vb[yk * 2 + cc, 0:HD, :] for yk in chips for cc in range(2)]
        spans = [
            jnp.concatenate(
                [
                    Vb[yk * 2 + cc, HD:VROWS, t * HD:(t + 1) * HD]
                    for cc in range(2) for t in range(2)
                ],
                axis=0,
            )
            for yk in chips
        ]
        mix = nn(
            jnp.concatenate(cached + spans, axis=1), Pw[0:len(chips) * 2 * (CTX + Q_DEV), :]
        )
        for _ in range(4):
            yield
        acc[xq] = acc[xq] * shrink + mix

    def together(*stages):
        stages = list(stages)
        while stages:
            stages = [s for s in stages if next(s, stages) is None]

    def wait_chip(pieces, k):
        for p in pieces:
            arrived(p, chip(k) * 2 + 1 - c)

    def pass_keys(p, d):
        yu, yd = around[-d], around[d]
        arrived(p, yu * 2 + c)
        piece(p, yu, 2).start()

        if d < 4:
            piece(p, yu, 0).start()
            arrived(p, yd * 2 + c)
            piece(p, yd, 2).start()

            if d < 3:
                piece(p, yd, 1).start()

    def pass_values(p, d):
        yu, yd = around[-d], around[d]
        arrived(p, yd * 2 + c)
        piece(p, yd, 2).start()

        if d < 4:
            piece(p, yd, 1).start()
            arrived(p, yu * 2 + c)
            piece(p, yu, 2).start()

            if d < 3:
                piece(p, yu, 0).start()

    def page_copy(j, yk):
        return remote(
            PKs.at[xs[j], yk], PKr.at[x, yk], sP.at[j, yk], rP.at[x, yk], xpeer[j]
        )

    def pages(k):
        yk = chip(k)
        r, tok = iota((32, CTX), 0), iota((32, CTX), 1)
        to = (y * 2 * NX + (r // 8) * 2 + c).astype(f32)
        got_k, got_v = [], []
        for cc in range(2):
            s = yk * 2 + cc
            meta = Kb[s, CTX + Q_DEV:KROWS, :].astype(f32)
            limit = jnp.concatenate([meta[0:1, :]] * 2, axis=1)
            route = jnp.concatenate([meta[1:2, :], meta[2:3, :]], axis=1)
            hit = (route == to) & (tok % 8 == r % 8) & (tok.astype(f32) < limit)
            one = jnp.where(hit, 1.0, 0.0).astype(bf16)
            got_k.append(nn(one, Kb[s, 0:CTX, :]))
            got_v.append(nt(one, Vb[s, 0:HD, :]))
            number = (inst(yk, x, cc) * PG + tok // PAGE + 1).astype(f32)
            found = jnp.sum(jnp.where(hit, number, 0.0), axis=1, keepdims=True) - 1.0
            here = iota((8, HD), 1) == inst(yk, x, cc)
            for v in range(NX):
                Is[v] = jnp.where(here, found[v * 8:v * 8 + 8, :].astype(i32), Is[v])
        for v in range(NX):
            for half, got in enumerate((got_k, got_v)):
                rows = jnp.concatenate([g[v * 8:v * 8 + 8, :] for g in got], axis=0)
                PKs[v, yk, half] = rows.astype(bf16)
        for j in (1, 2, 3):
            page_copy(j, yk).start()

    def send_ids():
        for j in (1, 2, 3):
            remote(Is.at[xs[j]], Ir.at[x], sI.at[j], rI.at[x], xpeer[j]).start()

    def out_copies(j):
        return (
            remote(Os.at[xs[j]], Or.at[x], sO.at[j], rO.at[x], xpeer[j]),
            remote(Ts.at[xs[j]], Tr.at[x], sT.at[j], rT.at[x], xpeer[j]),
        )

    def send_out(j):
        v = xs[j]
        Os[v] = acc[v].astype(bf16)
        top, total = m[v][0:1, :], jnp.sum(l[v], axis=0, keepdims=True)
        Ts[v] = jnp.concatenate(
            [row[:, t * HD:(t + 1) * HD] for row in (top, total) for t in range(R // HD)], axis=0
        )
        for copy in out_copies(j):
            copy.start()

    def decode_column():
        for k in range(8):
            arrived(4, chip(k) * 2 + 1 - c)
        o, peak, weight = merge(Db[...])
        DX[x, 0:8, :] = o
        DX[x, 8:16, :] = jnp.where(iota((8, HD), 1) < HD // 2, peak, weight)
        for j in (1, 2, 3):
            remote(DX.at[x], DX.at[x], sX.at[j], rX.at[x], xpeer[j]).start()

    def decode_project():
        for n in (5, 9, 10):
            loads[n].wait()
        for j in (1, 2, 3):
            remote(DX.at[xs[j]], DX.at[xs[j]], sX.at[j], rX.at[xs[j]], xpeer[j]).wait_recv()
        o, peak, weight = merge(DX[...])
        own = jnp.sum(dq.astype(f32) * nk_in[...].astype(f32), axis=1, keepdims=True) * SCALE
        last = jnp.maximum(peak, own)
        shrink, extra = jnp.exp2(peak - last), jnp.exp2(own - last)
        weight = weight * shrink + extra
        o = o * shrink + extra.astype(bf16).astype(f32) * nv_in[...].astype(f32)
        attended = (o / weight).astype(bf16).astype(f32)
        head = iota((G, HD), 0)
        wide = jnp.concatenate(
            [jnp.where(head == h, attended, 0.0) for h in range(G)], axis=1
        ).astype(bf16)
        Zb[z] = nn(wide, wb[...])
        for j, zz in enumerate(zpeers):
            remote(Zb.at[z], Zb.at[z], sZ.at[j], rZ.at[z], me, zz).start()

    def arrived_query(j):
        remote(Qb.at[xs[j]], Qb.at[xs[j]], sQ.at[j], rQ.at[xs[j]], xpeer[j]).wait_recv()

    def before(f):
        if f == 0:
            pass_values(2, 1)
            pass_values(3, 1)
        if f == 1:
            for k in (0, 1, 2):
                wait_chip((2, 3), k)
        if f in (2, 4, 7):
            pass_keys(0, f // 2 + 1 if f < 7 else 4)
            pass_keys(1, f // 2 + 1 if f < 7 else 4)
        if f == 2:
            for k in (0, 1, 2):
                pages(k)
            for k in (3, 4):
                wait_chip((0, 1), k)
        if f in (3, 6, 9):
            pass_values(2, f // 3 + 1)
            pass_values(3, f // 3 + 1)
        if f in (2, 5, 8, 10):
            pass_values(4, {2: 1, 5: 2, 8: 3, 10: 4}[f])
        if f == 4:
            arrived_query(3)
            for k in (3, 4):
                wait_chip((2, 3), k)
        if f == 5:
            pages(3)
            pages(4)
        if f == 6:
            for k in (5, 6):
                wait_chip((0, 1), k)
        if f == 8:
            for k in (5, 6):
                wait_chip((2, 3), k)
        if f == 9:
            wait_chip((0, 1), 7)
        if f == 10:
            pages(5)
            pages(6)
        if f == 11:
            wait_chip((2, 3), 7)
            decode_column()
        if f == 12:
            send_out(3)
            pages(7)
            send_ids()
        if f == 13:
            send_out(1)
        if f == 14:
            send_out(2)
            decode_project()

    pass_keys(0, 1)
    pass_keys(1, 1)
    arrived_query(1)
    for k in (0, 1, 2):
        wait_chip((0, 1), k)
    together(scores(0))
    arrived_query(2)
    end = len(UNITS)
    for f in range(end):
        before(f)
        stages = [values(f - 1)] if f else []
        stages.append(weights(f))
        if f + 1 < end:
            stages.append(scores(f + 1))
        together(*stages)
    together(values(end - 1))

    for j in (1, 2, 3):
        v = xs[j]
        for yk in range(NY):
            remote(
                PKs.at[v, yk], PKr.at[v, yk], sP.at[j, yk], rP.at[v, yk], xpeer[j]
            ).wait_recv()
        remote(Is.at[v], Ir.at[v], sI.at[j], rI.at[v], xpeer[j]).wait_recv()
    PKr[x] = PKs[x]
    Ir[x] = Is[x]
    stores = [
        pltpu.make_async_copy(PKr.at[v, :, half], ref.at[:, v], lsem.at[8 + half * NX + v])
        for half, ref in enumerate((hk_out, hv_out)) for v in range(NX)
    ]
    for store in stores:
        store.start()
    held = functools.reduce(jnp.maximum, [Ir[v] for v in range(NX)])
    held_stage[...] = held[0:1, 0:NX * NY * 2]
    stores.append(pltpu.make_async_copy(held_stage, ids_out, lsem.at[21]))
    stores[-1].start()

    for j, zz in enumerate(zpeers):
        remote(Zb.at[zz], Zb.at[zz], sZ.at[j], rZ.at[zz], me, zz).wait_recv()
    total = Zb[0]
    for v in range(1, nz):
        total = total + Zb[v]
    dec_stage[...] = jnp.sum(total, axis=0, keepdims=True).astype(bf16)
    stores.append(pltpu.make_async_copy(dec_stage, dec_out, lsem.at[22]))
    stores[-1].start()

    for j in (1, 2, 3):
        v = xs[j]
        remote(Os.at[v], Or.at[v], sO.at[j], rO.at[v], xpeer[j]).wait_recv()
        remote(Ts.at[v], Tr.at[v], sT.at[j], rT.at[v], xpeer[j]).wait_recv()
    def stat(j, first):
        return jnp.concatenate(
            [Tr[xs[j], first + t:first + t + 1, :] for t in range(R // HD)], axis=1
        )

    peaks = [m[x][0:1, :]] + [stat(j, 0) for j in (1, 2, 3)]
    sums = [jnp.sum(l[x], axis=0, keepdims=True)] + [stat(j, 4) for j in (1, 2, 3)]
    peak = functools.reduce(jnp.maximum, peaks)
    shares = [jnp.exp2(p - peak) for p in peaks]
    whole = sum(w * s for w, s in zip(shares, sums))
    shares = [w / whole for w in shares]
    mix = acc[x] * shares[0]
    for j in (1, 2, 3):
        mix = mix + Or[xs[j]].astype(f32) * shares[j]
    ostage[...] = mix.T.astype(bf16)
    done = pltpu.make_async_copy(ostage, out, lsem.at[7])
    done.start()

    for p in range(5):
        for d in range(4):
            if d == 0 and p < 2:
                continue
            if p < 2 or d < 3:
                piece(p, around[-d], 0).wait_send()
            if p > 1 or d < 3:
                piece(p, around[d], 1).wait_send()
        for yy in range(NY):
            piece(p, yy, 2).wait_send()
    span_copy.wait_send()
    for j in (1, 2, 3):
        if j == 3:
            qcopy(j).wait_send()
        for copy in out_copies(j):
            copy.wait_send()
        for yk in range(NY):
            page_copy(j, yk).wait_send()
        remote(Is.at[xs[j]], Ir.at[x], sI.at[j], rI.at[x], xpeer[j]).wait_send()
        remote(DX.at[x], DX.at[x], sX.at[j], rX.at[x], xpeer[j]).wait_send()
    for j, zz in enumerate(zpeers):
        remote(Zb.at[z], Zb.at[z], sZ.at[j], rZ.at[z], me, zz).wait_send()
    for store in stores:
        store.wait()
    done.wait()


def write(*refs):
    ins, outs, stages, sem = refs[:5], refs[5:10], refs[10:15], refs[15]
    first = [pltpu.make_async_copy(a, b, sem.at[0, n]) for n, (a, b) in enumerate(zip(ins, stages))]
    second = [pltpu.make_async_copy(a, b, sem.at[1, n]) for n, (a, b) in enumerate(zip(stages, outs))]
    for copy in first:
        copy.start()
    for copy, then in zip(first, second):
        copy.wait()
        then.start()
    for copy in second:
        copy.wait()


def local(
    nz,
    query, key_cache, value_cache, span_keys, span_values, live_pages, routes,
    decode_query, new_key, new_value, w_out,
):
    hbm = pl.BlockSpec(memory_space=pltpu.HBM)
    whole = pl.BlockSpec(memory_space=pl.ANY)
    V, D = pltpu.VMEM, pltpu.SemaphoreType.DMA
    out, hk, hv, ids, decoded = pl.pallas_call(
        functools.partial(kernel, nz),
        out_shape=(
            jax.ShapeDtypeStruct((R, HD), bf16),
            jax.ShapeDtypeStruct((NY, NX, 16, HD), bf16),
            jax.ShapeDtypeStruct((NY, NX, 16, HD), bf16),
            jax.ShapeDtypeStruct((1, NX * NY * 2), i32),
            jax.ShapeDtypeStruct((1, HD), bf16),
        ),
        in_specs=[hbm] * 11,
        out_specs=[whole] * 5,
        scratch_shapes=[
            V((1, 1), i32), V((1, PG), i32), V((G, HD), bf16), V((1, HD), bf16), V((1, HD), bf16),
            V((1, NX * NY * 2), i32), V((1, HD), bf16),
            V((2 * NY, KROWS, HD), bf16), V((2 * NY, VROWS, CTX), bf16), V((2 * NY, 16, HD), f32),
            V((NX, R, HD), bf16), V((CTX, HD), bf16), V((2, Q_DEV, HD), bf16),
            V((HD * G, HD), bf16),
            V((NX, HD, R), f32), V((NX, 8, R), f32), V((NX, 8, R), f32),
            V((N, R), f32), V((N, R), f32), V((N, R), bf16), V((N, R), bf16),
            V((8, R), f32), V((8, R), f32), V((8, R), f32), V((8, R), f32),
            V((NX, HD, R), bf16), V((NX, HD, R), bf16), V((NX, 8, HD), f32), V((NX, 8, HD), f32),
            V((NX, NY, 2, 16, HD), bf16), V((NX, NY, 2, 16, HD), bf16),
            V((NX, 8, HD), i32), V((NX, 8, HD), i32),
            V((NX, 16, HD), f32), V((nz, 8, HD), f32), V((R, HD), bf16),
            D((23,)),
            D((5, 3, NY)), D((5, 2 * NY)),
            D, D,
            D((NX,)), D((NX,)), D((NX,)), D((NX,)), D((NX,)), D((NX,)), D((NX, NY)), D((NX, NY)),
            D((NX,)), D((NX,)), D((NX,)), D((NX,)),
            D((nz,)), D((nz,)),
        ],
        compiler_params=pltpu.CompilerParams(
            collective_id=0, has_side_effects=True, vmem_limit_bytes=LIMIT
        ),
        cost_estimate=pl.CostEstimate(
            flops=4 * R * 64 * (CTX + Q_DEV) * HD, bytes_accessed=2**20,
            transcendentals=R * 64 * (CTX + Q_DEV),
        ),
        name="attend",
    )(
        query.reshape(R, HD), key_cache.reshape(CTX, HD), value_cache.reshape(CTX, HD),
        span_keys.reshape(Q_DEV, HD), span_values.reshape(Q_DEV, HD), w_out,
        live_pages.reshape(1, 1), routes.reshape(1, PG), decode_query, new_key, new_value,
    )
    results = (out, hk, hv, ids, decoded)
    out, hk, hv, ids, decoded = pl.pallas_call(
        write,
        out_shape=tuple(jax.ShapeDtypeStruct(a.shape, a.dtype) for a in results),
        in_specs=[whole] * 5,
        out_specs=[whole] * 5,
        scratch_shapes=[V(a.shape, a.dtype) for a in results] + [D((2, 5))],
        compiler_params=pltpu.CompilerParams(vmem_limit_bytes=LIMIT),
        name="write",
    )(*results)
    return (
        out.reshape(Q_DEV, G, HD),
        hk.reshape(NX * NY * 2, PAGE, 1, HD),
        hv.reshape(NX * NY * 2, PAGE, 1, HD),
        ids.reshape(NX * NY * 2),
        decoded,
    )


def solution(mesh):
    return jax.shard_map(
        functools.partial(local, mesh.shape["tp"]),
        mesh=mesh,
        in_specs=(
            P("inst", "tp", None),
            P("inst", "tp", None),
            P("inst", "tp", None),
            P("inst", "tp", None),
            P("inst", "tp", None),
            P("inst"),
            P("inst", None),
            P("tp", None),
            P("tp", None),
            P("tp", None),
            P("tp", "inst"),
        ),
        out_specs=(
            P("inst", "tp", None),
            P("inst", None, "tp", None),
            P("inst", None, "tp", None),
            P("inst"),
            P(None, "inst"),
        ),
        check_vma=False,
    )
```

```python
import functools
import math

import jax
import jax.numpy as jnp
from jax import lax
from jax.experimental import pallas as pl
from jax.experimental.pallas import tpu as pltpu
from jax.sharding import PartitionSpec as P

f32, bf16, i32 = jnp.float32, jnp.bfloat16, jnp.int32
MESH = pl.DeviceIdType.MESH
NEG = -1e30
LIMIT = 60 * 2**20
NX, NY = 4, 8
HD, G = 128, 8
Q_DEV, CTX, PAGE, PG = 64, 256, 8, 32
R = Q_DEV * G
KROWS = CTX + Q_DEV + 16
VROWS = HD + 32
N = 6 * (CTX + Q_DEV)
SCALE = math.log2(math.e) / math.sqrt(HD)


def nt(a, b):
    return lax.dot_general(a, b, (((1,), (1,)), ((), ())), preferred_element_type=f32)


def nn(a, b):
    return lax.dot_general(a, b, (((1,), (0,)), ((), ())), preferred_element_type=f32)


def iota(shape, dim):
    return lax.broadcasted_iota(i32, shape, dim)


NEAR, MID, FAR, LAST = (0, 1, 2), (3, 4), (5, 6), (7,)
UNITS = (
    (0, (0,)), (1, NEAR), (2, NEAR), (0, (1, 2)), (1, MID), (2, MID), (3, NEAR), (3, MID),
    (1, FAR), (2, FAR), (3, FAR), (3, LAST), (1, LAST), (2, LAST), (0, MID), (0, FAR + LAST),
)


def merge(parts):
    o, m, l = parts[:, 0:8], parts[:, 8:16, 0:1], parts[:, 8:16, HD // 2:HD // 2 + 1]
    peak = jnp.max(m, axis=0)
    w = jnp.exp2(m - peak[None])
    return jnp.sum(w * o, axis=0), peak, jnp.sum(w * l, axis=0)


def kernel(
    nz,
    q_in, kc_in, vc_in, sk_in, sv_in, w_in, live_hbm, routes_hbm, dq_hbm, nk_hbm, nv_hbm,
    out, hk_out, hv_out, ids_out, dec_out,
    live_in, routes_in, dq_in, nk_in, nv_in, held_stage, dec_stage, Kb, Vb, Db, Qb, vtmp, svb, wb, acc, m, l, Sa, Sb, Pa, Pb, al_a, al_b, mn_a, mn_b,
    Os, Or, Ts, Tr, PKs, PKr, Is, Ir, DX, Zb, ostage,
    lsem, sR, rR, sSV, rSV, sQ, rQ, sO, rO, sT, rT, sP, rP, sI, rI, sX, rX,
    sZ, rZ,
):
    me = lax.axis_index("inst")
    z = lax.axis_index("tp")
    c = me % 2
    x = (me // 2) % NX
    y = me // (2 * NX)

    def inst(yy, xx, cc):
        return (yy * NX + xx) * 2 + cc

    def ymod(v):
        return (v + 2 * NY) % NY

    sib = inst(y, x, 1 - c)
    up = inst(ymod(y + 1), x, c)
    down = inst(ymod(y - 1), x, c)
    xs = [x, (x + NX - 1) % NX, (x + 1) % NX, (x + 2) % NX]
    xpeer = [inst(y, v, c) for v in xs]
    mine = y * 2 + c

    around = [ymod(y + v) for v in range(NY)]

    def chip(k):
        return around[(4 if k == 7 else -((k + 1) // 2) if k % 2 else k // 2) % NY]

    def remote(src, dst, ss, rs, to, zz=None):
        return pltpu.make_async_remote_copy(
            src_ref=src, dst_ref=dst, send_sem=ss, recv_sem=rs,
            device_id=(to, z if zz is None else zz), device_id_type=MESH,
        )

    loads = [
        pltpu.make_async_copy(kc_in, Kb.at[mine, 0:CTX], lsem.at[0]),
        pltpu.make_async_copy(sk_in, Kb.at[mine, CTX:CTX + Q_DEV], lsem.at[1]),
        pltpu.make_async_copy(sv_in, svb.at[c], lsem.at[2]),
        pltpu.make_async_copy(q_in, Qb.at[x], lsem.at[3]),
        pltpu.make_async_copy(vc_in, vtmp, lsem.at[4]),
        pltpu.make_async_copy(w_in, wb, lsem.at[5]),
        pltpu.make_async_copy(live_hbm, live_in, lsem.at[16]),
        pltpu.make_async_copy(routes_hbm, routes_in, lsem.at[17]),
        pltpu.make_async_copy(dq_hbm, dq_in, lsem.at[18]),
        pltpu.make_async_copy(nk_hbm, nk_in, lsem.at[19]),
        pltpu.make_async_copy(nv_hbm, nv_in, lsem.at[20]),
    ]
    for load in loads:
        load.start()

    barrier = pltpu.get_barrier_semaphore()
    zpeers = [(z + j) % nz for j in range(1, nz)]
    for to in (sib, up, down, xpeer[1], xpeer[2], xpeer[3]):
        pl.semaphore_signal(barrier, inc=1, device_id=(to, z), device_id_type=MESH)
    for zz in zpeers:
        pl.semaphore_signal(barrier, inc=1, device_id=(me, zz), device_id_type=MESH)

    loads[6].wait()
    loads[7].wait()
    live_rows = live_in[0:1, 0:1] * PAGE
    wide = iota((PG, CTX), 1) // PAGE == iota((PG, CTX), 0)
    per_token = nn(
        jnp.broadcast_to(routes_in[...].astype(f32), (8, PG)).astype(bf16),
        jnp.where(wide, 1.0, 0.0).astype(bf16),
    )[0:1, :]
    row = iota((16, HD), 0)
    info = jnp.where(row == 0, live_rows.astype(f32), 0.0)
    info = jnp.where(row == 1, per_token[:, 0:HD], info)
    info = jnp.where(row == 2, per_token[:, HD:2 * HD], info)
    Kb[mine, CTX + Q_DEV:KROWS, :] = info.astype(bf16)
    for v in range(4):
        Is[v] = jnp.full((8, HD), -1, i32)
        m[v] = jnp.full((8, R), NEG, f32)
        l[v] = jnp.zeros((8, R), f32)
        acc[v] = jnp.zeros((HD, R), f32)

    loads[0].wait()
    loads[1].wait()
    loads[2].wait()
    loads[3].wait()
    pl.semaphore_wait(barrier, 6 + nz - 1)

    def piece(p, yy, way):
        part = (Kb, Vb, Db)[p].at[yy * 2 + c]
        return remote(
            part, part, sR.at[p, way, yy], rR.at[p, yy * 2 + c], (up, down, sib)[way]
        )

    def arrived(p, s):
        part = (Kb, Vb, Db)[p].at[s]
        remote(part, part, sR.at[p, 0, 0], rR.at[p, s], sib).wait_recv()

    def qcopy(j):
        return remote(Qb.at[x], Qb.at[x], sQ.at[j], rQ.at[x], xpeer[j])

    span_copy = remote(svb.at[c], svb.at[c], sSV, rSV, sib)
    span_copy.start()
    for way in (0, 1, 2):
        piece(0, y, way).start()
    qcopy(1).start()
    qcopy(2).start()
    loads[4].wait()
    Vb[mine, 0:HD, :] = vtmp[...].astype(f32).T.astype(bf16)
    remote(svb.at[1 - c], svb.at[1 - c], sSV, rSV, sib).wait_recv()
    both = jnp.concatenate([svb[0], svb[1]], axis=0).astype(f32).T
    half = jnp.where(c == 0, both[0:64], both[64:128])
    Vb[mine, HD:VROWS, :] = jnp.concatenate([half[0:32], half[32:64]], axis=1).astype(bf16)

    piece(1, y, 2).start()

    loads[8].wait()
    dq = dq_in[...]
    s_cache = nt(dq, Kb[mine, 0:CTX, :]) * SCALE
    s_cache = jnp.where(iota((G, CTX), 1) < live_rows, s_cache, NEG)
    s_span = nt(dq, Kb[mine, CTX:CTX + Q_DEV, :]) * SCALE
    peak = jnp.maximum(
        jnp.max(s_cache, axis=1, keepdims=True), jnp.max(s_span, axis=1, keepdims=True)
    )
    p_cache, p_span = jnp.exp2(s_cache - peak), jnp.exp2(s_span - peak)
    weight = jnp.sum(p_cache, axis=1, keepdims=True) + jnp.sum(p_span, axis=1, keepdims=True)
    mixed = nt(p_cache.astype(bf16), Vb[mine, 0:HD, :]) + nn(p_span.astype(bf16), svb[c])
    Db[mine, 0:8, :] = mixed
    Db[mine, 8:16, :] = jnp.where(iota((8, HD), 1) < HD // 2, peak, weight)

    bufs = ((Sa, Pa, al_a, mn_a), (Sb, Pb, al_b, mn_b))

    def scores(f):
        block, chips = UNITS[f]
        S, _, al, mn = bufs[f % 2]
        xq, chips = xs[block], [chip(k) for k in chips]
        q = Qb[xq]
        top, at = None, 0
        for yk in chips:
            for cc in range(2):
                s = yk * 2 + cc
                limit = Kb[s, CTX + Q_DEV:KROWS, :].astype(f32)[0:1, :]
                sc = nt(Kb[s, 0:CTX, :], q)
                ok = iota((CTX, HD), 0).astype(f32) < limit
                sc = jnp.concatenate(
                    [jnp.where(ok, sc[:, t * HD:(t + 1) * HD], NEG) for t in range(R // HD)],
                    axis=1,
                )
                S[at:at + CTX, :] = sc
                at += CTX
                best = jnp.max(sc.reshape(CTX // 8, 8, R), axis=0)
                top = best if top is None else jnp.maximum(top, best)
                yield
        for yk in chips:
            keys = jnp.concatenate(
                [Kb[yk * 2, CTX:CTX + Q_DEV, :], Kb[yk * 2 + 1, CTX:CTX + Q_DEV, :]], axis=0
            )
            sc = nt(keys, q)
            ahead = (inst(y, xq, c) - inst(yk, x, 0)) * Q_DEV
            sc = jnp.where(iota((HD, R), 0) <= iota((HD, R), 1) // G + ahead, sc, NEG)
            S[at:at + HD, :] = sc
            at += HD
            top = jnp.maximum(top, jnp.max(sc.reshape(HD // 8, 8, R), axis=0))
        yield
        old = m[xq]
        new = jnp.maximum(old, jnp.max(top, axis=0, keepdims=True) * SCALE)
        al[...] = jnp.exp2(old - new)
        mn[...] = new
        m[xq] = new

    def weights(f):
        block, chips = UNITS[f]
        S, Pw, al, mn = bufs[f % 2]
        xq = xs[block]
        shrink, peak = al[...], mn[0:1, :]
        total = None
        rows = len(chips) * 2 * (CTX + Q_DEV)
        for at in range(0, rows, CTX):
            n = min(CTX, rows - at)
            p = jnp.exp2(S[at:at + n, :] * SCALE - peak)
            Pw[at:at + n, :] = p.astype(bf16)
            part = jnp.sum(p.reshape(n // 8, 8, R), axis=0)
            total = part if total is None else total + part
            yield
        l[xq] = l[xq] * shrink + total

    def values(f):
        block, chips = UNITS[f]
        _, Pw, al, _ = bufs[f % 2]
        xq, chips = xs[block], [chip(k) for k in chips]
        shrink = al[0:1, :]
        cached = [Vb[yk * 2 + cc, 0:HD, :] for yk in chips for cc in range(2)]
        spans = [
            jnp.concatenate(
                [
                    Vb[yk * 2 + cc, HD:VROWS, t * HD:(t + 1) * HD]
                    for cc in range(2) for t in range(2)
                ],
                axis=0,
            )
            for yk in chips
        ]
        mix = nn(
            jnp.concatenate(cached + spans, axis=1), Pw[0:len(chips) * 2 * (CTX + Q_DEV), :]
        )
        for _ in range(4):
            yield
        acc[xq] = acc[xq] * shrink + mix

    def together(*stages):
        stages = list(stages)
        while stages:
            stages = [s for s in stages if next(s, stages) is None]

    def wait_chip(pieces, k):
        for p in pieces:
            arrived(p, chip(k) * 2 + 1 - c)

    def pass_keys(d, p=0):
        yu, yd = around[-d], around[d]
        arrived(p, yu * 2 + c)
        piece(p, yu, 2).start()

        if d < 4:
            piece(p, yu, 0).start()
            arrived(p, yd * 2 + c)
            piece(p, yd, 2).start()

            if d < 3:
                piece(p, yd, 1).start()

    def pass_values(d, p=1):
        yu, yd = around[-d], around[d]
        arrived(p, yd * 2 + c)
        piece(p, yd, 2).start()

        if d < 4:
            piece(p, yd, 1).start()
            arrived(p, yu * 2 + c)
            piece(p, yu, 2).start()

            if d < 3:
                piece(p, yu, 0).start()

    def page_copy(j, yk):
        return remote(
            PKs.at[xs[j], yk], PKr.at[x, yk], sP.at[j, yk], rP.at[x, yk], xpeer[j]
        )

    def pages(k):
        yk = chip(k)
        r, tok = iota((32, CTX), 0), iota((32, CTX), 1)
        to = (y * 2 * NX + (r // 8) * 2 + c).astype(f32)
        got_k, got_v = [], []
        for cc in range(2):
            s = yk * 2 + cc
            meta = Kb[s, CTX + Q_DEV:KROWS, :].astype(f32)
            limit = jnp.concatenate([meta[0:1, :]] * 2, axis=1)
            route = jnp.concatenate([meta[1:2, :], meta[2:3, :]], axis=1)
            hit = (route == to) & (tok % 8 == r % 8) & (tok.astype(f32) < limit)
            one = jnp.where(hit, 1.0, 0.0).astype(bf16)
            got_k.append(nn(one, Kb[s, 0:CTX, :]))
            got_v.append(nt(one, Vb[s, 0:HD, :]))
            yield
            number = (inst(yk, x, cc) * PG + tok // PAGE + 1).astype(f32)
            found = jnp.sum(jnp.where(hit, number, 0.0), axis=1, keepdims=True) - 1.0
            here = iota((8, HD), 1) == inst(yk, x, cc)
            for v in range(NX):
                Is[v] = jnp.where(here, found[v * 8:v * 8 + 8, :].astype(i32), Is[v])
        for v in range(NX):
            for half, got in enumerate((got_k, got_v)):
                rows = jnp.concatenate([g[v * 8:v * 8 + 8, :] for g in got], axis=0)
                PKs[v, yk, half] = rows.astype(bf16)
        for j in (1, 2, 3):
            page_copy(j, yk).start()

    def send_ids():
        for j in (1, 2, 3):
            remote(Is.at[xs[j]], Ir.at[x], sI.at[j], rI.at[x], xpeer[j]).start()

    def out_copies(j):
        return (
            remote(Ts.at[xs[j]], Tr.at[x], sT.at[j], rT.at[x], xpeer[j]),
            remote(Os.at[xs[j]], Or.at[x], sO.at[j], rO.at[x], xpeer[j]),
        )

    def send_out(j):
        v = xs[j]
        Os[v] = acc[v].astype(bf16)
        top, total = m[v][0:1, :], jnp.sum(l[v], axis=0, keepdims=True)
        Ts[v] = jnp.concatenate(
            [row[:, t * HD:(t + 1) * HD] for row in (top, total) for t in range(R // HD)], axis=0
        )
        for copy in out_copies(j):
            copy.start()

    def decode_column():
        for k in range(8):
            arrived(2, chip(k) * 2 + 1 - c)
        o, peak, weight = merge(Db[...])
        DX[x, 0:8, :] = o
        DX[x, 8:16, :] = jnp.where(iota((8, HD), 1) < HD // 2, peak, weight)
        for j in (1, 2, 3):
            remote(DX.at[x], DX.at[x], sX.at[j], rX.at[x], xpeer[j]).start()

    def decode_project():
        for n in (5, 9, 10):
            loads[n].wait()
        for j in (1, 2, 3):
            remote(DX.at[xs[j]], DX.at[xs[j]], sX.at[j], rX.at[xs[j]], xpeer[j]).wait_recv()
        o, peak, weight = merge(DX[...])
        own = jnp.sum(dq.astype(f32) * nk_in[...].astype(f32), axis=1, keepdims=True) * SCALE
        last = jnp.maximum(peak, own)
        shrink, extra = jnp.exp2(peak - last), jnp.exp2(own - last)
        weight = weight * shrink + extra
        o = o * shrink + extra.astype(bf16).astype(f32) * nv_in[...].astype(f32)
        attended = (o / weight).astype(bf16).astype(f32)
        head = iota((G, HD), 0)
        wide = jnp.concatenate(
            [jnp.where(head == h, attended, 0.0) for h in range(G)], axis=1
        ).astype(bf16)
        Zb[z] = nn(wide, wb[...])
        for j, zz in enumerate(zpeers):
            remote(Zb.at[z], Zb.at[z], sZ.at[j], rZ.at[z], me, zz).start()

    def arrived_query(j):
        remote(Qb.at[xs[j]], Qb.at[xs[j]], sQ.at[j], rQ.at[xs[j]], xpeer[j]).wait_recv()

    def before(f):
        if f == 1:
            pass_values(1)
        if f == 2:
            for k in (1, 2):
                wait_chip((1,), k)
        if f in (3, 5, 8):
            pass_keys({3: 2, 5: 3, 8: 4}[f])
        if f in (3, 6, 9):
            pass_values(f // 3 + 1)
        if f in (3, 6, 9, 11):
            pass_values({3: 1, 6: 2, 9: 3, 11: 4}[f], 2)
        if f == 3:
            for k in (3, 4):
                wait_chip((0,), k)
        if f == 5:
            arrived_query(3)
            for k in (3, 4):
                wait_chip((1,), k)
        if f == 7:
            for k in (5, 6):
                wait_chip((0,), k)
        if f == 9:
            for k in (5, 6):
                wait_chip((1,), k)
        if f == 10:
            wait_chip((0,), 7)
        if f == 12:
            wait_chip((1,), 7)
        if f == 13:
            send_out(3)
        if f == 14:
            send_out(1)
        if f == 15:
            send_out(2)
            send_ids()
            decode_column()

    wait_chip((0,), 0)
    together(scores(0))
    for p in (1, 2):
        if p == 1:
            for way in (0, 1):
                piece(0, y, way).wait_send()
        for way in (0, 1, 2):
            if p == 2 or way < 2:
                piece(p, y, way).start()
    wait_chip((1,), 0)
    together(weights(0), pages(0))
    qcopy(1).wait_send()
    qcopy(2).wait_send()
    qcopy(3).start()
    pass_keys(1)
    arrived_query(1)
    for k in (1, 2):
        wait_chip((0,), k)
    together(values(0), scores(1))
    arrived_query(2)
    end = len(UNITS)
    beside = {3: (1, 2), 6: (3, 4), 10: (5, 6), 14: (7,)}
    for f in range(1, end):
        before(f)
        stages = [values(f - 1)] if f > 1 else []
        stages.append(weights(f))
        if f + 1 < end:
            stages.append(scores(f + 1))
        together(*stages, *(pages(k) for k in beside.get(f, ())))
    together(values(end - 1))
    decode_project()

    for j in (1, 2, 3):
        v = xs[j]
        for yk in range(NY):
            remote(
                PKs.at[v, yk], PKr.at[v, yk], sP.at[j, yk], rP.at[v, yk], xpeer[j]
            ).wait_recv()
        remote(Is.at[v], Ir.at[v], sI.at[j], rI.at[v], xpeer[j]).wait_recv()
    PKr[x] = PKs[x]
    Ir[x] = Is[x]
    stores = [
        pltpu.make_async_copy(PKr.at[v, :, half], ref.at[:, v], lsem.at[8 + half * NX + v])
        for half, ref in enumerate((hk_out, hv_out)) for v in range(NX)
    ]
    for store in stores:
        store.start()
    held = functools.reduce(jnp.maximum, [Ir[v] for v in range(NX)])
    held_stage[...] = held[0:1, 0:NX * NY * 2]
    stores.append(pltpu.make_async_copy(held_stage, ids_out, lsem.at[21]))
    stores[-1].start()

    for j, zz in enumerate(zpeers):
        remote(Zb.at[zz], Zb.at[zz], sZ.at[j], rZ.at[zz], me, zz).wait_recv()
    total = Zb[0]
    for v in range(1, nz):
        total = total + Zb[v]
    dec_stage[...] = jnp.sum(total, axis=0, keepdims=True).astype(bf16)
    stores.append(pltpu.make_async_copy(dec_stage, dec_out, lsem.at[22]))
    stores[-1].start()

    for p in range(3):
        for d in range(4):
            if d == 0 and p == 0:
                continue
            if p == 0 or d < 3:
                piece(p, around[-d], 0).wait_send()
            if p > 0 or d < 3:
                piece(p, around[d], 1).wait_send()
        for yy in range(NY):
            piece(p, yy, 2).wait_send()
    span_copy.wait_send()
    qcopy(3).wait_send()
    for j in (1, 2, 3):
        for yk in range(NY):
            page_copy(j, yk).wait_send()
        remote(Is.at[xs[j]], Ir.at[x], sI.at[j], rI.at[x], xpeer[j]).wait_send()
        remote(DX.at[x], DX.at[x], sX.at[j], rX.at[x], xpeer[j]).wait_send()
    for j, zz in enumerate(zpeers):
        remote(Zb.at[z], Zb.at[z], sZ.at[j], rZ.at[z], me, zz).wait_send()

    for j in (1, 2, 3):
        v = xs[j]
        remote(Ts.at[v], Tr.at[v], sT.at[j], rT.at[v], xpeer[j]).wait_recv()

    def stat(j, first):
        return jnp.concatenate(
            [Tr[xs[j], first + t:first + t + 1, :] for t in range(R // HD)], axis=1
        )

    peaks = [m[x][0:1, :]] + [stat(j, 0) for j in (1, 2, 3)]
    sums = [jnp.sum(l[x], axis=0, keepdims=True)] + [stat(j, 4) for j in (1, 2, 3)]
    peak = functools.reduce(jnp.maximum, peaks)
    shares = [jnp.exp2(p - peak) for p in peaks]
    whole = sum(w * s for w, s in zip(shares, sums))
    shares = [w / whole for w in shares]
    mix = acc[x] * shares[0]
    for j in (1, 2, 3):
        v = xs[j]
        remote(Os.at[v], Or.at[v], sO.at[j], rO.at[v], xpeer[j]).wait_recv()
        mix = mix + Or[v].astype(f32) * shares[j]
    ostage[...] = mix.T.astype(bf16)
    done = pltpu.make_async_copy(ostage, out, lsem.at[7])
    done.start()

    for j in (1, 2, 3):
        for copy in out_copies(j):
            copy.wait_send()
    for store in stores:
        store.wait()
    done.wait()


def write(*refs):
    ins, outs, stages, sem = refs[:5], refs[5:10], refs[10:15], refs[15]
    first = [pltpu.make_async_copy(a, b, sem.at[0, n]) for n, (a, b) in enumerate(zip(ins, stages))]
    second = [pltpu.make_async_copy(a, b, sem.at[1, n]) for n, (a, b) in enumerate(zip(stages, outs))]
    for copy in first:
        copy.start()
    for copy, then in zip(first, second):
        copy.wait()
        then.start()
    for copy in second:
        copy.wait()


def local(
    nz,
    query, key_cache, value_cache, span_keys, span_values, live_pages, routes,
    decode_query, new_key, new_value, w_out,
):
    hbm = pl.BlockSpec(memory_space=pltpu.HBM)
    whole = pl.BlockSpec(memory_space=pl.ANY)
    V, D = pltpu.VMEM, pltpu.SemaphoreType.DMA
    out, hk, hv, ids, decoded = pl.pallas_call(
        functools.partial(kernel, nz),
        out_shape=(
            jax.ShapeDtypeStruct((R, HD), bf16),
            jax.ShapeDtypeStruct((NY, NX, 16, HD), bf16),
            jax.ShapeDtypeStruct((NY, NX, 16, HD), bf16),
            jax.ShapeDtypeStruct((1, NX * NY * 2), i32),
            jax.ShapeDtypeStruct((1, HD), bf16),
        ),
        in_specs=[hbm] * 11,
        out_specs=[whole] * 5,
        scratch_shapes=[
            V((1, 1), i32), V((1, PG), i32), V((G, HD), bf16), V((1, HD), bf16), V((1, HD), bf16),
            V((1, NX * NY * 2), i32), V((1, HD), bf16),
            V((2 * NY, KROWS, HD), bf16), V((2 * NY, VROWS, CTX), bf16), V((2 * NY, 16, HD), f32),
            V((NX, R, HD), bf16), V((CTX, HD), bf16), V((2, Q_DEV, HD), bf16),
            V((HD * G, HD), bf16),
            V((NX, HD, R), f32), V((NX, 8, R), f32), V((NX, 8, R), f32),
            V((N, R), f32), V((N, R), f32), V((N, R), bf16), V((N, R), bf16),
            V((8, R), f32), V((8, R), f32), V((8, R), f32), V((8, R), f32),
            V((NX, HD, R), bf16), V((NX, HD, R), bf16), V((NX, 8, HD), f32), V((NX, 8, HD), f32),
            V((NX, NY, 2, 16, HD), bf16), V((NX, NY, 2, 16, HD), bf16),
            V((NX, 8, HD), i32), V((NX, 8, HD), i32),
            V((NX, 16, HD), f32), V((nz, 8, HD), f32), V((R, HD), bf16),
            D((23,)),
            D((3, 3, NY)), D((3, 2 * NY)),
            D, D,
            D((NX,)), D((NX,)), D((NX,)), D((NX,)), D((NX,)), D((NX,)), D((NX, NY)), D((NX, NY)),
            D((NX,)), D((NX,)), D((NX,)), D((NX,)),
            D((nz,)), D((nz,)),
        ],
        compiler_params=pltpu.CompilerParams(
            collective_id=0, has_side_effects=True, vmem_limit_bytes=LIMIT
        ),
        cost_estimate=pl.CostEstimate(
            flops=4 * R * 64 * (CTX + Q_DEV) * HD, bytes_accessed=2**20,
            transcendentals=R * 64 * (CTX + Q_DEV),
        ),
        name="attend",
    )(
        query.reshape(R, HD), key_cache.reshape(CTX, HD), value_cache.reshape(CTX, HD),
        span_keys.reshape(Q_DEV, HD), span_values.reshape(Q_DEV, HD), w_out,
        live_pages.reshape(1, 1), routes.reshape(1, PG), decode_query, new_key, new_value,
    )
    results = (out, hk, hv, ids, decoded)
    out, hk, hv, ids, decoded = pl.pallas_call(
        write,
        out_shape=tuple(jax.ShapeDtypeStruct(a.shape, a.dtype) for a in results),
        in_specs=[whole] * 5,
        out_specs=[whole] * 5,
        scratch_shapes=[V(a.shape, a.dtype) for a in results] + [D((2, 5))],
        compiler_params=pltpu.CompilerParams(vmem_limit_bytes=LIMIT),
        name="write",
    )(*results)
    return (
        out.reshape(Q_DEV, G, HD),
        hk.reshape(NX * NY * 2, PAGE, 1, HD),
        hv.reshape(NX * NY * 2, PAGE, 1, HD),
        ids.reshape(NX * NY * 2),
        decoded,
    )


def solution(mesh):
    return jax.shard_map(
        functools.partial(local, mesh.shape["tp"]),
        mesh=mesh,
        in_specs=(
            P("inst", "tp", None),
            P("inst", "tp", None),
            P("inst", "tp", None),
            P("inst", "tp", None),
            P("inst", "tp", None),
            P("inst"),
            P("inst", None),
            P("tp", None),
            P("tp", None),
            P("tp", None),
            P("tp", "inst"),
        ),
        out_specs=(
            P("inst", "tp", None),
            P("inst", None, "tp", None),
            P("inst", None, "tp", None),
            P("inst"),
            P(None, "inst"),
        ),
        check_vma=False,
    )
```

```python
import functools
import math

import jax
import jax.numpy as jnp
from jax import lax
from jax.experimental import pallas as pl
from jax.experimental.pallas import tpu as pltpu
from jax.sharding import PartitionSpec as P

f32, bf16, i32 = jnp.float32, jnp.bfloat16, jnp.int32
MESH = pl.DeviceIdType.MESH
NEG = -1e30
LIMIT = 60 * 2**20
NX, NY = 4, 8
HD, G = 128, 8
Q_DEV, CTX, PAGE, PG = 64, 256, 8, 32
R = Q_DEV * G
KROWS = CTX + Q_DEV + 16
VROWS = HD + 32
N = 6 * (CTX + Q_DEV)
SCALE = math.log2(math.e) / math.sqrt(HD)


def nt(a, b):
    return lax.dot_general(a, b, (((1,), (1,)), ((), ())), preferred_element_type=f32)


def nn(a, b):
    return lax.dot_general(a, b, (((1,), (0,)), ((), ())), preferred_element_type=f32)


def iota(shape, dim):
    return lax.broadcasted_iota(i32, shape, dim)


NEAR, MID, FAR, LAST = (0, 1, 2), (3, 4), (5, 6), (7,)
UNITS = (
    (0, (0,)), (1, NEAR), (2, NEAR), (0, (1, 2)), (1, MID), (2, MID), (3, NEAR), (3, MID),
    (1, FAR), (2, FAR), (3, FAR), (3, LAST), (1, LAST), (2, LAST), (0, MID), (0, FAR + LAST),
)


def merge(parts):
    o, m, l = parts[:, 0:8], parts[:, 8:16, 0:1], parts[:, 8:16, HD // 2:HD // 2 + 1]
    peak = jnp.max(m, axis=0)
    w = jnp.exp2(m - peak[None])
    return jnp.sum(w * o, axis=0), peak, jnp.sum(w * l, axis=0)


def kernel(
    nz,
    q_in, kc_in, vc_in, sk_in, sv_in, w_in, live_hbm, routes_hbm, dq_hbm, nk_hbm, nv_hbm,
    out, hk_out, hv_out, ids_out, dec_out,
    live_in, routes_in, dq_in, nk_in, nv_in, held_stage, dec_stage, Kb, Vb, Db, Qb, vtmp, svb, wb, acc, m, l, Sa, Sb, Pa, Pb, al_a, al_b, mn_a, mn_b,
    Os, Or, Ts, Tr, PKs, PKr, Is, Ir, DX, Zb, ostage,
    lsem, sR, rR, sSV, rSV, sQ, rQ, sO, rO, sT, rT, sP, rP, sI, rI, sX, rX,
    sZ, rZ,
):
    me = lax.axis_index("inst")
    z = lax.axis_index("tp")
    c = me % 2
    x = (me // 2) % NX
    y = me // (2 * NX)

    def inst(yy, xx, cc):
        return (yy * NX + xx) * 2 + cc

    def ymod(v):
        return (v + 2 * NY) % NY

    sib = inst(y, x, 1 - c)
    up = inst(ymod(y + 1), x, c)
    down = inst(ymod(y - 1), x, c)
    xs = [x, (x + NX - 1) % NX, (x + 1) % NX, (x + 2) % NX]
    xpeer = [inst(y, v, c) for v in xs]
    mine = y * 2 + c

    around = [ymod(y + v) for v in range(NY)]

    def chip(k):
        return around[(4 if k == 7 else -((k + 1) // 2) if k % 2 else k // 2) % NY]

    def remote(src, dst, ss, rs, to, zz=None):
        return pltpu.make_async_remote_copy(
            src_ref=src, dst_ref=dst, send_sem=ss, recv_sem=rs,
            device_id=(to, z if zz is None else zz), device_id_type=MESH,
        )

    loads = [
        pltpu.make_async_copy(kc_in, Kb.at[mine, 0:CTX], lsem.at[0]),
        pltpu.make_async_copy(sk_in, Kb.at[mine, CTX:CTX + Q_DEV], lsem.at[1]),
        pltpu.make_async_copy(sv_in, svb.at[c], lsem.at[2]),
        pltpu.make_async_copy(q_in, Qb.at[x], lsem.at[3]),
        pltpu.make_async_copy(vc_in, vtmp, lsem.at[4]),
        pltpu.make_async_copy(w_in, wb, lsem.at[5]),
        pltpu.make_async_copy(live_hbm, live_in, lsem.at[16]),
        pltpu.make_async_copy(routes_hbm, routes_in, lsem.at[17]),
        pltpu.make_async_copy(dq_hbm, dq_in, lsem.at[18]),
        pltpu.make_async_copy(nk_hbm, nk_in, lsem.at[19]),
        pltpu.make_async_copy(nv_hbm, nv_in, lsem.at[20]),
    ]
    for load in loads:
        load.start()

    barrier = pltpu.get_barrier_semaphore()
    zpeers = [(z + j) % nz for j in range(1, nz)]
    for to in (sib, up, down, xpeer[1], xpeer[2], xpeer[3]):
        pl.semaphore_signal(barrier, inc=1, device_id=(to, z), device_id_type=MESH)
    for zz in zpeers:
        pl.semaphore_signal(barrier, inc=1, device_id=(me, zz), device_id_type=MESH)

    loads[6].wait()
    loads[7].wait()
    live_rows = live_in[0:1, 0:1] * PAGE
    wide = iota((PG, CTX), 1) // PAGE == iota((PG, CTX), 0)
    per_token = nn(
        jnp.broadcast_to(routes_in[...].astype(f32), (8, PG)).astype(bf16),
        jnp.where(wide, 1.0, 0.0).astype(bf16),
    )[0:1, :]
    row = iota((16, HD), 0)
    info = jnp.where(row == 0, live_rows.astype(f32), 0.0)
    info = jnp.where(row == 1, per_token[:, 0:HD], info)
    info = jnp.where(row == 2, per_token[:, HD:2 * HD], info)
    Kb[mine, CTX + Q_DEV:KROWS, :] = info.astype(bf16)
    for v in range(4):
        Is[v] = jnp.full((8, HD), -1, i32)
        m[v] = jnp.full((8, R), NEG, f32)
        l[v] = jnp.zeros((8, R), f32)
        acc[v] = jnp.zeros((HD, R), f32)

    loads[0].wait()
    loads[1].wait()
    loads[2].wait()
    loads[3].wait()
    pl.semaphore_wait(barrier, 6 + nz - 1)

    def piece(p, yy, way):
        part = (Kb, Vb, Db)[p].at[yy * 2 + c]
        return remote(
            part, part, sR.at[p, way, yy], rR.at[p, yy * 2 + c], (up, down, sib)[way]
        )

    def arrived(p, s):
        part = (Kb, Vb, Db)[p].at[s]
        remote(part, part, sR.at[p, 0, 0], rR.at[p, s], sib).wait_recv()

    def qcopy(j):
        return remote(Qb.at[x], Qb.at[x], sQ.at[j], rQ.at[x], xpeer[j])

    span_copy = remote(svb.at[c], svb.at[c], sSV, rSV, sib)
    span_copy.start()
    for way in (0, 1, 2):
        piece(0, y, way).start()
    qcopy(1).start()
    qcopy(2).start()
    loads[4].wait()
    Vb[mine, 0:HD, :] = vtmp[...].astype(f32).T.astype(bf16)
    remote(svb.at[1 - c], svb.at[1 - c], sSV, rSV, sib).wait_recv()
    both = jnp.concatenate([svb[0], svb[1]], axis=0).astype(f32).T
    half = jnp.where(c == 0, both[0:64], both[64:128])
    Vb[mine, HD:VROWS, :] = jnp.concatenate([half[0:32], half[32:64]], axis=1).astype(bf16)

    piece(1, y, 2).start()

    loads[8].wait()
    dq = dq_in[...]
    s_cache = nt(dq, Kb[mine, 0:CTX, :]) * SCALE
    s_cache = jnp.where(iota((G, CTX), 1) < live_rows, s_cache, NEG)
    s_span = nt(dq, Kb[mine, CTX:CTX + Q_DEV, :]) * SCALE
    peak = jnp.maximum(
        jnp.max(s_cache, axis=1, keepdims=True), jnp.max(s_span, axis=1, keepdims=True)
    )
    p_cache, p_span = jnp.exp2(s_cache - peak), jnp.exp2(s_span - peak)
    weight = jnp.sum(p_cache, axis=1, keepdims=True) + jnp.sum(p_span, axis=1, keepdims=True)
    mixed = nt(p_cache.astype(bf16), Vb[mine, 0:HD, :]) + nn(p_span.astype(bf16), svb[c])
    Db[mine, 0:8, :] = mixed
    Db[mine, 8:16, :] = jnp.where(iota((8, HD), 1) < HD // 2, peak, weight)

    bufs = ((Sa, Pa, al_a, mn_a), (Sb, Pb, al_b, mn_b))

    def scores(f):
        block, chips = UNITS[f]
        S, _, al, mn = bufs[f % 2]
        xq, chips = xs[block], [chip(k) for k in chips]
        q = Qb[xq]
        top, at = None, 0
        for yk in chips:
            for cc in range(2):
                s = yk * 2 + cc
                limit = Kb[s, CTX + Q_DEV:KROWS, :].astype(f32)[0:1, :]
                sc = nt(Kb[s, 0:CTX, :], q)
                ok = iota((CTX, HD), 0).astype(f32) < limit
                sc = jnp.concatenate(
                    [jnp.where(ok, sc[:, t * HD:(t + 1) * HD], NEG) for t in range(R // HD)],
                    axis=1,
                )
                S[at:at + CTX, :] = sc
                at += CTX
                best = jnp.max(sc.reshape(CTX // 8, 8, R), axis=0)
                top = best if top is None else jnp.maximum(top, best)
                yield
        for yk in chips:
            keys = jnp.concatenate(
                [Kb[yk * 2, CTX:CTX + Q_DEV, :], Kb[yk * 2 + 1, CTX:CTX + Q_DEV, :]], axis=0
            )
            sc = nt(keys, q)
            ahead = (inst(y, xq, c) - inst(yk, x, 0)) * Q_DEV
            sc = jnp.where(iota((HD, R), 0) <= iota((HD, R), 1) // G + ahead, sc, NEG)
            S[at:at + HD, :] = sc
            at += HD
            top = jnp.maximum(top, jnp.max(sc.reshape(HD // 8, 8, R), axis=0))
        yield
        old = m[xq]
        new = jnp.maximum(old, jnp.max(top, axis=0, keepdims=True) * SCALE)
        al[...] = jnp.exp2(old - new)
        mn[...] = new
        m[xq] = new

    def weights(f):
        block, chips = UNITS[f]
        S, Pw, al, mn = bufs[f % 2]
        xq = xs[block]
        shrink, peak = al[...], mn[0:1, :]
        total = None
        rows = len(chips) * 2 * (CTX + Q_DEV)
        for at in range(0, rows, CTX):
            n = min(CTX, rows - at)
            p = jnp.exp2(S[at:at + n, :] * SCALE - peak)
            Pw[at:at + n, :] = p.astype(bf16)
            part = jnp.sum(p.reshape(n // 8, 8, R), axis=0)
            total = part if total is None else total + part
            yield
        l[xq] = l[xq] * shrink + total

    def values(f):
        block, chips = UNITS[f]
        _, Pw, al, _ = bufs[f % 2]
        xq, chips = xs[block], [chip(k) for k in chips]
        shrink = al[0:1, :]
        cached = [Vb[yk * 2 + cc, 0:HD, :] for yk in chips for cc in range(2)]
        spans = [
            jnp.concatenate(
                [
                    Vb[yk * 2 + cc, HD:VROWS, t * HD:(t + 1) * HD]
                    for cc in range(2) for t in range(2)
                ],
                axis=0,
            )
            for yk in chips
        ]
        mix = nn(
            jnp.concatenate(cached + spans, axis=1), Pw[0:len(chips) * 2 * (CTX + Q_DEV), :]
        )
        for _ in range(4):
            yield
        acc[xq] = acc[xq] * shrink + mix

    def together(*stages):
        stages = list(stages)
        while stages:
            stages = [s for s in stages if next(s, stages) is None]

    def wait_chip(pieces, k):
        for p in pieces:
            arrived(p, chip(k) * 2 + 1 - c)

    def pass_keys(d, p=0):
        yu, yd = around[-d], around[d]
        arrived(p, yu * 2 + c)
        piece(p, yu, 2).start()

        if d < 4:
            piece(p, yu, 0).start()
            arrived(p, yd * 2 + c)
            piece(p, yd, 2).start()

            if d < 3:
                piece(p, yd, 1).start()

    def pass_values(d, p=1):
        yu, yd = around[-d], around[d]
        arrived(p, yd * 2 + c)
        piece(p, yd, 2).start()

        if d < 4:
            piece(p, yd, 1).start()
            arrived(p, yu * 2 + c)
            piece(p, yu, 2).start()

            if d < 3:
                piece(p, yu, 0).start()

    def page_copy(j, yk):
        return remote(
            PKs.at[xs[j], yk], PKr.at[x, yk], sP.at[j, yk], rP.at[x, yk], xpeer[j]
        )

    def pages(k):
        yk = chip(k)
        r, tok = iota((32, CTX), 0), iota((32, CTX), 1)
        to = (y * 2 * NX + (r // 8) * 2 + c).astype(f32)
        got_k, got_v = [], []
        for cc in range(2):
            s = yk * 2 + cc
            meta = Kb[s, CTX + Q_DEV:KROWS, :].astype(f32)
            limit = jnp.concatenate([meta[0:1, :]] * 2, axis=1)
            route = jnp.concatenate([meta[1:2, :], meta[2:3, :]], axis=1)
            hit = (route == to) & (tok % 8 == r % 8) & (tok.astype(f32) < limit)
            one = jnp.where(hit, 1.0, 0.0).astype(bf16)
            got_k.append(nn(one, Kb[s, 0:CTX, :]))
            got_v.append(nt(one, Vb[s, 0:HD, :]))
            yield
            number = (inst(yk, x, cc) * PG + tok // PAGE + 1).astype(f32)
            found = jnp.sum(jnp.where(hit, number, 0.0), axis=1, keepdims=True) - 1.0
            here = iota((8, HD), 1) == inst(yk, x, cc)
            for v in range(NX):
                Is[v] = jnp.where(here, found[v * 8:v * 8 + 8, :].astype(i32), Is[v])
        for v in range(NX):
            for half, got in enumerate((got_k, got_v)):
                rows = jnp.concatenate([g[v * 8:v * 8 + 8, :] for g in got], axis=0)
                PKs[v, yk, half] = rows.astype(bf16)
        for j in (1, 2, 3):
            page_copy(j, yk).start()

    def send_ids():
        for j in (1, 2, 3):
            remote(Is.at[xs[j]], Ir.at[x], sI.at[j], rI.at[x], xpeer[j]).start()

    def out_copies(j):
        return (
            remote(Ts.at[xs[j]], Tr.at[x], sT.at[j], rT.at[x], xpeer[j]),
            remote(Os.at[xs[j]], Or.at[x], sO.at[j], rO.at[x], xpeer[j]),
        )

    def send_out(j):
        v = xs[j]
        Os[v] = acc[v].astype(bf16)
        top, total = m[v][0:1, :], jnp.sum(l[v], axis=0, keepdims=True)
        Ts[v] = jnp.concatenate(
            [row[:, t * HD:(t + 1) * HD] for row in (top, total) for t in range(R // HD)], axis=0
        )
        for copy in out_copies(j):
            copy.start()

    def decode_column():
        for k in range(8):
            arrived(2, chip(k) * 2 + 1 - c)
        o, peak, weight = merge(Db[...])
        DX[x, 0:8, :] = o
        DX[x, 8:16, :] = jnp.where(iota((8, HD), 1) < HD // 2, peak, weight)
        for j in (1, 2, 3):
            remote(DX.at[x], DX.at[x], sX.at[j], rX.at[x], xpeer[j]).start()

    def decode_project():
        for n in (5, 9, 10):
            loads[n].wait()
        for j in (1, 2, 3):
            remote(DX.at[xs[j]], DX.at[xs[j]], sX.at[j], rX.at[xs[j]], xpeer[j]).wait_recv()
        o, peak, weight = merge(DX[...])
        own = jnp.sum(dq.astype(f32) * nk_in[...].astype(f32), axis=1, keepdims=True) * SCALE
        last = jnp.maximum(peak, own)
        shrink, extra = jnp.exp2(peak - last), jnp.exp2(own - last)
        weight = weight * shrink + extra
        o = o * shrink + extra.astype(bf16).astype(f32) * nv_in[...].astype(f32)
        attended = (o / weight).astype(bf16).astype(f32)
        head = iota((G, HD), 0)
        wide = jnp.concatenate(
            [jnp.where(head == h, attended, 0.0) for h in range(G)], axis=1
        ).astype(bf16)
        Zb[z] = nn(wide, wb[...])
        for j, zz in enumerate(zpeers):
            remote(Zb.at[z], Zb.at[z], sZ.at[j], rZ.at[z], me, zz).start()

    def arrived_query(j):
        remote(Qb.at[xs[j]], Qb.at[xs[j]], sQ.at[j], rQ.at[xs[j]], xpeer[j]).wait_recv()

    def before(f):
        if f == 1:
            pass_values(1)
        if f == 2:
            for k in (1, 2):
                wait_chip((1,), k)
        if f in (3, 5, 8):
            pass_keys({3: 2, 5: 3, 8: 4}[f])
        if f in (3, 6, 9):
            pass_values(f // 3 + 1)
        if f in (3, 6, 9, 11):
            pass_values({3: 1, 6: 2, 9: 3, 11: 4}[f], 2)
        if f == 3:
            for k in (3, 4):
                wait_chip((0,), k)
        if f == 5:
            arrived_query(3)
            for k in (3, 4):
                wait_chip((1,), k)
        if f == 7:
            for k in (5, 6):
                wait_chip((0,), k)
        if f == 9:
            for k in (5, 6):
                wait_chip((1,), k)
        if f == 10:
            wait_chip((0,), 7)
        if f == 12:
            wait_chip((1,), 7)
        if f == 13:
            send_out(3)
            decode_column()
        if f == 14:
            send_out(1)
        if f == 15:
            send_out(2)
            send_ids()
            decode_project()

    wait_chip((0,), 0)
    together(scores(0))
    for p in (1, 2):
        if p == 1:
            for way in (0, 1):
                piece(0, y, way).wait_send()
        for way in (0, 1, 2):
            if p == 2 or way < 2:
                piece(p, y, way).start()
    wait_chip((1,), 0)
    together(weights(0), pages(0))
    qcopy(1).wait_send()
    qcopy(2).wait_send()
    qcopy(3).start()
    pass_keys(1)
    arrived_query(1)
    for k in (1, 2):
        wait_chip((0,), k)
    together(values(0), scores(1))
    arrived_query(2)
    end = len(UNITS)
    beside = {3: (1, 2), 6: (3, 4), 10: (5, 6), 14: (7,)}
    for f in range(1, end):
        before(f)
        stages = [values(f - 1)] if f > 1 else []
        stages.append(weights(f))
        if f + 1 < end:
            stages.append(scores(f + 1))
        together(*stages, *(pages(k) for k in beside.get(f, ())))
    together(values(end - 1))

    for j in (1, 2, 3):
        v = xs[j]
        for yk in range(NY):
            remote(
                PKs.at[v, yk], PKr.at[v, yk], sP.at[j, yk], rP.at[v, yk], xpeer[j]
            ).wait_recv()
        remote(Is.at[v], Ir.at[v], sI.at[j], rI.at[v], xpeer[j]).wait_recv()
    PKr[x] = PKs[x]
    Ir[x] = Is[x]
    stores = [
        pltpu.make_async_copy(PKr.at[v, :, half], ref.at[:, v], lsem.at[8 + half * NX + v])
        for half, ref in enumerate((hk_out, hv_out)) for v in range(NX)
    ]
    for store in stores:
        store.start()
    held = functools.reduce(jnp.maximum, [Ir[v] for v in range(NX)])
    held_stage[...] = held[0:1, 0:NX * NY * 2]
    stores.append(pltpu.make_async_copy(held_stage, ids_out, lsem.at[21]))
    stores[-1].start()

    for p in range(3):
        for d in range(4):
            if d == 0 and p == 0:
                continue
            if p == 0 or d < 3:
                piece(p, around[-d], 0).wait_send()
            if p > 0 or d < 3:
                piece(p, around[d], 1).wait_send()
        for yy in range(NY):
            piece(p, yy, 2).wait_send()
    span_copy.wait_send()
    qcopy(3).wait_send()
    for j in (1, 2, 3):
        for yk in range(NY):
            page_copy(j, yk).wait_send()
        remote(Is.at[xs[j]], Ir.at[x], sI.at[j], rI.at[x], xpeer[j]).wait_send()
        remote(DX.at[x], DX.at[x], sX.at[j], rX.at[x], xpeer[j]).wait_send()
    for j, zz in enumerate(zpeers):
        remote(Zb.at[z], Zb.at[z], sZ.at[j], rZ.at[z], me, zz).wait_send()

    for j in (1, 2, 3):
        v = xs[j]
        remote(Ts.at[v], Tr.at[v], sT.at[j], rT.at[v], xpeer[j]).wait_recv()

    def stat(j, first):
        return jnp.concatenate(
            [Tr[xs[j], first + t:first + t + 1, :] for t in range(R // HD)], axis=1
        )

    peaks = [m[x][0:1, :]] + [stat(j, 0) for j in (1, 2, 3)]
    sums = [jnp.sum(l[x], axis=0, keepdims=True)] + [stat(j, 4) for j in (1, 2, 3)]
    peak = functools.reduce(jnp.maximum, peaks)
    shares = [jnp.exp2(p - peak) for p in peaks]
    whole = sum(w * s for w, s in zip(shares, sums))
    shares = [w / whole for w in shares]
    mix = acc[x] * shares[0]
    for j in (1, 2, 3):
        v = xs[j]
        remote(Os.at[v], Or.at[v], sO.at[j], rO.at[v], xpeer[j]).wait_recv()
        mix = mix + Or[v].astype(f32) * shares[j]
    ostage[...] = mix.T.astype(bf16)
    done = pltpu.make_async_copy(ostage, out, lsem.at[7])
    done.start()

    for j, zz in enumerate(zpeers):
        remote(Zb.at[zz], Zb.at[zz], sZ.at[j], rZ.at[zz], me, zz).wait_recv()
    total = Zb[0]
    for v in range(1, nz):
        total = total + Zb[v]
    dec_stage[...] = jnp.sum(total, axis=0, keepdims=True).astype(bf16)
    stores.append(pltpu.make_async_copy(dec_stage, dec_out, lsem.at[22]))
    stores[-1].start()

    for j in (1, 2, 3):
        for copy in out_copies(j):
            copy.wait_send()
    for store in stores:
        store.wait()
    done.wait()


def write(*refs):
    ins, outs, stages, sem = refs[:5], refs[5:10], refs[10:15], refs[15]
    first = [pltpu.make_async_copy(a, b, sem.at[0, n]) for n, (a, b) in enumerate(zip(ins, stages))]
    second = [pltpu.make_async_copy(a, b, sem.at[1, n]) for n, (a, b) in enumerate(zip(stages, outs))]
    for copy in first:
        copy.start()
    for copy, then in zip(first, second):
        copy.wait()
        then.start()
    for copy in second:
        copy.wait()


def local(
    nz,
    query, key_cache, value_cache, span_keys, span_values, live_pages, routes,
    decode_query, new_key, new_value, w_out,
):
    hbm = pl.BlockSpec(memory_space=pltpu.HBM)
    whole = pl.BlockSpec(memory_space=pl.ANY)
    V, D = pltpu.VMEM, pltpu.SemaphoreType.DMA
    out, hk, hv, ids, decoded = pl.pallas_call(
        functools.partial(kernel, nz),
        out_shape=(
            jax.ShapeDtypeStruct((R, HD), bf16),
            jax.ShapeDtypeStruct((NY, NX, 16, HD), bf16),
            jax.ShapeDtypeStruct((NY, NX, 16, HD), bf16),
            jax.ShapeDtypeStruct((1, NX * NY * 2), i32),
            jax.ShapeDtypeStruct((1, HD), bf16),
        ),
        in_specs=[hbm] * 11,
        out_specs=[whole] * 5,
        scratch_shapes=[
            V((1, 1), i32), V((1, PG), i32), V((G, HD), bf16), V((1, HD), bf16), V((1, HD), bf16),
            V((1, NX * NY * 2), i32), V((1, HD), bf16),
            V((2 * NY, KROWS, HD), bf16), V((2 * NY, VROWS, CTX), bf16), V((2 * NY, 16, HD), f32),
            V((NX, R, HD), bf16), V((CTX, HD), bf16), V((2, Q_DEV, HD), bf16),
            V((HD * G, HD), bf16),
            V((NX, HD, R), f32), V((NX, 8, R), f32), V((NX, 8, R), f32),
            V((N, R), f32), V((N, R), f32), V((N, R), bf16), V((N, R), bf16),
            V((8, R), f32), V((8, R), f32), V((8, R), f32), V((8, R), f32),
            V((NX, HD, R), bf16), V((NX, HD, R), bf16), V((NX, 8, HD), f32), V((NX, 8, HD), f32),
            V((NX, NY, 2, 16, HD), bf16), V((NX, NY, 2, 16, HD), bf16),
            V((NX, 8, HD), i32), V((NX, 8, HD), i32),
            V((NX, 16, HD), f32), V((nz, 8, HD), f32), V((R, HD), bf16),
            D((23,)),
            D((3, 3, NY)), D((3, 2 * NY)),
            D, D,
            D((NX,)), D((NX,)), D((NX,)), D((NX,)), D((NX,)), D((NX,)), D((NX, NY)), D((NX, NY)),
            D((NX,)), D((NX,)), D((NX,)), D((NX,)),
            D((nz,)), D((nz,)),
        ],
        compiler_params=pltpu.CompilerParams(
            collective_id=0, has_side_effects=True, vmem_limit_bytes=LIMIT
        ),
        cost_estimate=pl.CostEstimate(
            flops=4 * R * 64 * (CTX + Q_DEV) * HD, bytes_accessed=2**20,
            transcendentals=R * 64 * (CTX + Q_DEV),
        ),
        name="attend",
    )(
        query.reshape(R, HD), key_cache.reshape(CTX, HD), value_cache.reshape(CTX, HD),
        span_keys.reshape(Q_DEV, HD), span_values.reshape(Q_DEV, HD), w_out,
        live_pages.reshape(1, 1), routes.reshape(1, PG), decode_query, new_key, new_value,
    )
    results = (out, hk, hv, ids, decoded)
    out, hk, hv, ids, decoded = pl.pallas_call(
        write,
        out_shape=tuple(jax.ShapeDtypeStruct(a.shape, a.dtype) for a in results),
        in_specs=[whole] * 5,
        out_specs=[whole] * 5,
        scratch_shapes=[V(a.shape, a.dtype) for a in results] + [D((2, 5))],
        compiler_params=pltpu.CompilerParams(vmem_limit_bytes=LIMIT),
        name="write",
    )(*results)
    return (
        out.reshape(Q_DEV, G, HD),
        hk.reshape(NX * NY * 2, PAGE, 1, HD),
        hv.reshape(NX * NY * 2, PAGE, 1, HD),
        ids.reshape(NX * NY * 2),
        decoded,
    )


def solution(mesh):
    return jax.shard_map(
        functools.partial(local, mesh.shape["tp"]),
        mesh=mesh,
        in_specs=(
            P("inst", "tp", None),
            P("inst", "tp", None),
            P("inst", "tp", None),
            P("inst", "tp", None),
            P("inst", "tp", None),
            P("inst"),
            P("inst", None),
            P("tp", None),
            P("tp", None),
            P("tp", None),
            P("tp", "inst"),
        ),
        out_specs=(
            P("inst", "tp", None),
            P("inst", None, "tp", None),
            P("inst", None, "tp", None),
            P("inst"),
            P(None, "inst"),
        ),
        check_vma=False,
    )
```
